128 devices in a mesh: member: 4 (over x), grid: 32 (over y, z, core).
Axes of the slice: x: 4, y: 4, z: 4, core: 2. Of those that a mesh axis runs over, the one named last changes fastest.
Arguments:
- predictions: float32 [8, 100, 65536], P('member', None, 'grid'), may hold values from -6 to 6
- target: float32 [100, 65536], P(None, 'grid'), may hold values from -6 to 6
- area: float32 [65536], P('grid'), may hold values from 0.3 to 3
- var_weight: float32 [100], replicated, may hold values from 0.3 to 3
- pre_act: bfloat16 [8, 65536, 1024], P('member', 'grid'), may hold values from -6 to 6
- latent: bfloat16 [8, 8192, 1024], P('member', 'grid'), may hold values from -6 to 6
- w_hidden: bfloat16 [1024, 1024], replicated, may hold values from -0.1875 to 0.1875
- w_out: bfloat16 [1024, 100], replicated, may hold values from -0.1875 to 0.1875
- edge_slot: int32 [65536, 4], P('grid'), may hold values from 0 to 383, as said below
- edge_count: int32 [65536], P('grid'), may hold values from 3 to 4
- edge_coef: bfloat16 [65536, 4], P('grid'), may hold values from 0.19921875 to 1
- send_next: int32 [2048], P('grid'), may hold values from 0 to 255, as said below
- send_prev: int32 [2048], P('grid'), may hold values from 0 to 255, as said below
Outputs:
- grad_latent: float32 [8, 8192, 1024], P('member', 'grid')
- grad_w_hidden: float32 [1024, 1024], P(('member', 'grid'))
- grad_w_out: float32 [1024, 100], replicated
The draws below stay inside these ranges and needn't reach their ends.
Inputs may be any that keep to these rules, and one draw needn't show every extreme that they name: `edge_slot`: the 4 slots of a point name distinct rows of its shard's extended table. `send_next`: within each shard's block of 64 entries the rows are distinct. `send_prev`: within each shard's block of 64 entries the rows are distinct.
All inputs are finite; a program needn't handle non-finite values.
Results may differ from the reference program's by a relative error of at most 0.005.
Values may be sent and summed in bfloat16 or wider, within the bound.
A program may use at most 128 MiB of HBM per device.

```python
import math
import jax
import jax.numpy as jnp
from jax import lax

MEMBERS = 8
LAT = 1024
VARS = 100
EDGES = 4
PTS_DEV = 2048
MESH_DEV = 256
HALO = 64
EXT = 384
POINTS = 65536
MESH = 8192


def draw_edge_slot(key, part):
    key = jax.random.fold_in(key, 11)
    first, second = jax.random.split(key)
    base = jax.random.randint(first, (POINTS, 1), 0, EXT)
    stride = jax.random.randint(second, (POINTS, 1), 1, (EXT - 1) // 3 + 1)
    steps = jnp.arange(EDGES, dtype=jnp.int32)[None, :]
    return ((base + steps * stride) % EXT).astype(jnp.int32)


def lent_rows(key):
    shards = MESH // MESH_DEV
    keys = jax.random.split(key, shards)
    rows = jax.vmap(lambda each: jax.random.permutation(each, MESH_DEV)[:HALO])(keys)
    return rows.reshape(shards * HALO).astype(jnp.int32)


def draw_send_next(key, part):
    key = jax.random.fold_in(key, 23)
    return lent_rows(key)


def draw_send_prev(key, part):
    key = jax.random.fold_in(key, 37)
    return lent_rows(key)


def plant(drawn, stream_key, least, high):
    spot = [jax.random.randint(jax.random.fold_in(stream_key, axis), (), 0, length) for axis, length in enumerate(drawn.shape)]
    main_axis = drawn.shape.index(max(drawn.shape))
    next_to = spot[:main_axis] + [(spot[main_axis] + 1) % drawn.shape[main_axis]] + spot[main_axis + 1:]
    return drawn.at[tuple(spot)].set(least).at[tuple(next_to)].set(high)


def block_scale(rng, extent, cuts, low, high):
    def one(position, shards_of):
        heights = jax.random.uniform(jax.random.fold_in(jax.random.fold_in(rng, 6), position), (shards_of,), jnp.float32, low / len(cuts), high / len(cuts))
        return jnp.repeat(jnp.exp(heights), extent[position] // shards_of).reshape((-1,) + (1,) * (len(extent) - position - 1))

    level = one(*cuts[0])
    for cut in cuts[1:]:
        level = level * one(*cut)
    return level


def scatter_about(own_key, extent, scale, most, pieces=(), kind=jnp.bfloat16):
    values = jax.random.normal(own_key, extent, jnp.float32) * scale
    if len(pieces) > 0:
        values = block_scale(own_key, extent, pieces, -0.22, 0.18) * values
    return jnp.clip(values, min=-most, max=most).astype(kind)


def setup_inputs(seed: int = 0) -> dict:
    streams_of = jax.random.split(jax.random.key(seed), 14)
    return {
        "predictions": scatter_about(streams_of[0], (MEMBERS, VARS, POINTS), 1.0, 6.0, ((0, 4), (2, 32)), jnp.float32),
        "target": scatter_about(streams_of[1], (VARS, POINTS), 1.0, 6.0, ((1, 32),), jnp.float32),
        "area": jnp.clip(jnp.exp(math.log(3.0) - 2.3025851 * jax.random.uniform(streams_of[2], (POINTS,), jnp.float32) ** block_scale(streams_of[2], (POINTS,), ((0, 32),), -0.2, 0.2)), 0.3, 3.0),
        "var_weight": jnp.clip(jnp.exp(jax.random.uniform(streams_of[3], (VARS,), jnp.float32, math.log(0.3), math.log(3.0))), 0.3, 3.0),
        "pre_act": scatter_about(streams_of[4], (MEMBERS, POINTS, LAT), 1.0, 6.0, ((0, 4), (1, 32))),
        "latent": scatter_about(streams_of[5], (MEMBERS, MESH, LAT), 1.0, 6.0, ((0, 4), (1, 32))),
        "w_hidden": scatter_about(streams_of[6], (LAT, LAT), LAT ** -0.5, 0.1875),
        "w_out": scatter_about(streams_of[7], (LAT, VARS), LAT ** -0.5, 0.1875),
        "edge_slot": draw_edge_slot(jax.random.fold_in(streams_of[13], 71), 0),
        "edge_count": plant(jax.random.randint(streams_of[9], (POINTS,), 3, 5), jax.random.fold_in(streams_of[9], 1), 3, 4).astype(jnp.int32),
        "edge_coef": jnp.clip(0.19921875 + 0.80078125 * jax.random.uniform(streams_of[10], (POINTS, EDGES), jnp.float32) ** block_scale(streams_of[10], (POINTS, EDGES), ((0, 32),), -0.2, 0.2), 0.19921875, 1.0).astype(jnp.bfloat16),
        "send_next": draw_send_next(jax.random.fold_in(streams_of[13], 71), 0),
        "send_prev": draw_send_prev(jax.random.fold_in(streams_of[13], 71), 0),
    }


def crps_grad(own, every, tgt, area, var_weight, count):
    direct = jnp.sign(own - tgt[None]) / count
    pair = jnp.zeros(own.shape, jnp.float32)
    for other in range(every.shape[0]):
        pair = pair + jnp.sign(own - every[other][None])
    return area[None, None, :] * var_weight[None, :, None] * (direct - pair / (count * (count - 1)))

def edge_matrix(slots, counts, coefs, rows):
    column = jnp.arange(rows, dtype=jnp.int32)
    total = jnp.zeros((slots.shape[0], rows), jnp.float32)
    for slot in range(slots.shape[1]):
        used = jnp.where(counts > slot, coefs[:, slot].astype(jnp.float32), 0.0)
        total = total + jnp.where(slots[:, slot][:, None] == column[None, :], used[:, None], 0.0)
    return total

def reference(predictions, target, area, var_weight, pre_act, latent, w_hidden, w_out, edge_slot, edge_count, edge_coef, send_next, send_prev):
    shards = MESH // MESH_DEV
    grad_y = crps_grad(predictions, predictions, target, area, var_weight, MEMBERS).astype(jnp.bfloat16)
    lat = latent.reshape(MEMBERS, shards, MESH_DEV, LAT)
    next_rows = send_next.reshape(shards, HALO)
    prev_rows = send_prev.reshape(shards, HALO)
    pick = jax.vmap(lambda rows, index: rows[:, index], in_axes=(1, 0), out_axes=1)
    lent_next = pick(lat, next_rows)
    lent_prev = pick(lat, prev_rows)
    blank = jnp.zeros((MEMBERS, 1, HALO, LAT), jnp.bfloat16)
    from_prev = jnp.concatenate([blank, lent_next[:, :-1]], axis=1)
    from_next = jnp.concatenate([lent_prev[:, 1:], blank], axis=1)
    ext = jnp.concatenate([lat, from_prev, from_next], axis=2)
    ext_s = jnp.moveaxis(ext, 1, 0)
    pre_s = jnp.moveaxis(pre_act.reshape(MEMBERS, shards, PTS_DEV, LAT), 1, 0)
    dy_s = jnp.moveaxis(grad_y.reshape(MEMBERS, VARS, shards, PTS_DEV), 2, 0)
    slot_s = edge_slot.reshape(shards, PTS_DEV, EDGES)
    count_s = edge_count.reshape(shards, PTS_DEV)
    coef_s = edge_coef.reshape(shards, PTS_DEV, EDGES)
    w_hid = w_hidden.astype(jnp.float32)
    w_o = w_out.astype(jnp.float32)
    hp = lax.Precision.HIGHEST

    def one_shard(carry, items):
        total_w1, total_w2 = carry
        table, pre, grad_out, slots, counts, coefs = items
        weights = edge_matrix(slots, counts, coefs, EXT)
        agg = jnp.einsum('pe,mel->mpl', weights, table.astype(jnp.float32), precision=hp).astype(jnp.bfloat16)
        pre32 = pre.astype(jnp.float32)
        hidden = jax.nn.gelu(pre32).astype(jnp.bfloat16)
        dy32 = grad_out.astype(jnp.float32)
        dhid = jnp.einsum('mvp,lv->mpl', dy32, w_o, precision=hp)
        dpre = jax.vjp(jax.nn.gelu, pre32)[1](dhid)[0].astype(jnp.bfloat16)
        total_w2 = total_w2 + jnp.einsum('mpl,mvp->lv', hidden.astype(jnp.float32), dy32, precision=hp)
        total_w1 = total_w1 + jnp.einsum('mpl,mpk->lk', agg.astype(jnp.float32), dpre.astype(jnp.float32), precision=hp)
        dagg = jnp.einsum('mpk,lk->mpl', dpre.astype(jnp.float32), w_hid, precision=hp).astype(jnp.bfloat16)
        dext = jnp.einsum('pe,mpl->mel', weights, dagg.astype(jnp.float32), precision=hp)
        return ((total_w1, total_w2), dext)
    start = (jnp.zeros((LAT, LAT), jnp.float32), jnp.zeros((LAT, VARS), jnp.float32))
    (total_w1, total_w2), dext = lax.scan(one_shard, start, (ext_s, pre_s, dy_s, slot_s, count_s, coef_s))
    own = dext[:, :, :MESH_DEV]
    zero = jnp.zeros((1, MEMBERS, HALO, LAT), jnp.float32)
    back_a = jnp.concatenate([dext[1:, :, MESH_DEV:MESH_DEV + HALO], zero], axis=0)
    back_b = jnp.concatenate([zero, dext[:-1, :, MESH_DEV + HALO:]], axis=0)
    place = jax.vmap(lambda base, index, rows: base.at[:, index].add(rows))
    own = place(own, next_rows, back_a)
    own = place(own, prev_rows, back_b)
    grad_latent = jnp.moveaxis(own, 0, 1).reshape(MEMBERS, MESH, LAT)
    scale = 1.0 / math.sqrt(MEMBERS * POINTS)
    return (grad_latent, total_w1 * scale, total_w2 * scale)
```

```python
import functools
import math

import jax
import jax.numpy as jnp
from jax import lax
from jax.experimental import pallas as pl
from jax.experimental.pallas import tpu as pltpu
from jax.sharding import PartitionSpec as P

MESH_ID = pl.DeviceIdType.MESH
C_GELU = math.sqrt(2.0 / math.pi)
A_GELU = 0.044715
CH = 128
BF = jnp.bfloat16
F32 = jnp.float32


def column_parts(lat):
    tiles = lat // 128
    sizes = [tiles // 3 + (1 if i < tiles % 3 else 0) for i in range(3)]
    parts, start = [], 0
    for size in sizes:
        parts.append((start * 128, size * 128))
        start += size
    return parts


def dot(a, b, dims=((1,), (0,))):
    return lax.dot_general(a, b, (dims, ((), ())), preferred_element_type=F32)


class Sizes:
    def __init__(self, mesh, predictions, pre_act, latent, send_next):
        self.nx = mesh.shape["member"]
        self.grid = mesh.shape["grid"]
        chips = self.grid // 2
        self.ny = math.isqrt(chips)
        self.nz = chips // self.ny
        self.ml, self.nv, self.npts = predictions.shape
        self.lat = pre_act.shape[2]
        self.rows = latent.shape[1]
        self.halo = send_next.shape[0]
        self.ext = self.rows + 2 * self.halo
        self.qn = self.npts // self.nx
        self.nc = self.qn // CH
        self.vfull = self.nv // 16 * 16
        self.vp = -(-self.nv // 16) * 16
        self.rpd = self.lat // (self.nx * self.grid)
        self.members = self.nx * self.ml
        self.gcol = self.lat // 2 // self.nz
        self.parts = column_parts(self.lat)
        self.total = self.members * self.npts * self.grid


AXIS_ORDERS = ((2, 1, 0), (1, 0, 2), (0, 2, 1))


def kernel(sz, *refs):
    it = iter(refs)
    preds, target, area, vweight, pre, latent, w_hidden, w_out = [next(it) for _ in range(8)]
    slots, counts, coefs, next_rows, prev_rows = [next(it) for _ in range(5)]
    out_lat, out_wh, out_wo = [next(it) for _ in range(3)]
    lat_v, wh_v, wo_v, tgt_v = [next(it) for _ in range(4)]
    rb, dyo, dyb, pbuf, hid, dg, st, wot = [next(it) for _ in range(8)]
    q, qb, g, ext_t = [next(it) for _ in range(4)]
    lent_s, lent_r, back_r, gl = [next(it) for _ in range(4)]
    score = [next(it) for _ in range(3)]
    rcore = [next(it) for _ in range(3)]
    r1 = [next(it) for _ in range(3)]
    s1 = [next(it) for _ in range(3)]
    v1 = [next(it) for _ in range(3)]
    r2 = [next(it) for _ in range(3)]
    s2 = [next(it) for _ in range(3)]
    v2 = [next(it) for _ in range(3)]
    r3 = [next(it) for _ in range(3)]
    v3 = [next(it) for _ in range(3)]
    g_cs, g_cr, gh, gz_s, gz_r, gy, gx, gfin = [next(it) for _ in range(8)]
    loc_sem, own_sem, pre_sem, tgt_sem, out_sem = [next(it) for _ in range(5)]
    f_s, f_r, b_s, b_r, h_s, h_r, k_s, k_r = [next(it) for _ in range(8)]
    c_s, c_r, a_s, a_r, g_s, g_r = [next(it) for _ in range(6)]

    nx, ny, nz, ml, nv, lat = sz.nx, sz.ny, sz.nz, sz.ml, sz.nv, sz.lat
    nc, qn, ext, rows, halo = sz.nc, sz.qn, sz.ext, sz.rows, sz.halo
    dims = (nx, ny, nz)
    x = lax.axis_index("member")
    s = lax.axis_index("grid")
    core = lax.rem(s, 2)
    z = lax.rem(lax.div(s, 2), nz)
    y = lax.div(s, 2 * nz)
    other = 1 - core
    coord = (x, y, z)

    def device(cx, cy, cz, cc):
        return (cx, (cy * nz + cz) * 2 + cc)

    def peer(axis, by):
        there = list(coord)
        there[axis] = lax.rem(coord[axis] + by, dims[axis])
        return there[axis], device(*there, core)

    mate = device(x, y, z, other)
    behind = (x, lax.rem(s + sz.grid - 1, sz.grid))
    ahead = (x, lax.rem(s + 1, sz.grid))

    def remote(src, dst, send_sem, recv_sem, to):
        return pltpu.make_async_remote_copy(
            src_ref=src, dst_ref=dst, send_sem=send_sem, recv_sem=recv_sem, device_id=to, device_id_type=MESH_ID
        )

    def own_copy(c):
        return pltpu.make_async_copy(
            preds.at[:, :, pl.ds(pl.multiple_of(x * qn + c * CH, CH), CH)], rb.at[c, 0], own_sem.at[c]
        )

    def tgt_copy(c):
        return pltpu.make_async_copy(
            target.at[:, pl.ds(pl.multiple_of(x * qn + c * CH, CH), CH)], tgt_v.at[c], tgt_sem.at[c]
        )

    def forward(c, o):
        there, to = peer(0, o)
        return remote(
            preds.at[:, :, pl.ds(pl.multiple_of(there * qn + c * CH, CH), CH)],
            rb.at[c, o],
            f_s.at[c, o - 1],
            f_r.at[c, o - 1],
            to,
        )

    def backward(c, o):
        _, to = peer(0, nx - o)
        return remote(dyo.at[c, o - 1], dyb.at[c, o], b_s.at[c, o - 1], b_r.at[c, o - 1], to)

    blocks = nc * nx * ml
    depth = pbuf.shape[0]

    def pre_copy(i):
        m = lax.rem(i, ml)
        o = lax.rem(lax.div(i, ml), nx)
        c = lax.div(i, ml * nx)
        quarter = lax.rem(x + o, nx)
        slot = lax.rem(i, depth)
        return pltpu.make_async_copy(
            pre.at[m, pl.ds(pl.multiple_of(quarter * qn + c * CH, CH), CH), :], pbuf.at[slot], pre_sem.at[slot]
        )

    lat_copy = pltpu.make_async_copy(latent, lat_v, loc_sem.at[0])
    wo_copy = pltpu.make_async_copy(w_out, wo_v, loc_sem.at[1])
    wh_copy = pltpu.make_async_copy(w_hidden, wh_v, loc_sem.at[2])

    lat_copy.start()
    for i in range(depth):
        pre_copy(i).start()

    barrier = pltpu.get_barrier_semaphore()
    neighbours = [peer(a, o)[1] for a in range(3) for o in range(1, dims[a])] + [behind, ahead]
    for to in neighbours:
        pl.semaphore_signal(barrier, inc=1, device_id=to, device_id_type=MESH_ID)
    pl.semaphore_wait(barrier, len(neighbours))

    for c in range(nc):
        for o in range(1, nx):
            forward(c, o).start()
        own_copy(c).start()
        tgt_copy(c).start()
    wo_copy.start()
    wh_copy.start()

    lat_copy.wait()
    line = lax.broadcasted_iota(jnp.int32, (rows, halo), 0)
    pick_next = jnp.where(line == next_rows[...], 1.0, 0.0).astype(BF)
    pick_prev = jnp.where(line == prev_rows[...], 1.0, 0.0).astype(BF)
    for m in range(ml):
        lent_s[0, m] = dot(pick_next, lat_v[m], ((0,), (0,))).astype(BF)
        lent_s[1, m] = dot(pick_prev, lat_v[m], ((0,), (0,))).astype(BF)
    lend_a = remote(lent_s.at[0], lent_r.at[0], h_s.at[0], h_r.at[0], ahead)
    lend_b = remote(lent_s.at[1], lent_r.at[1], h_s.at[1], h_r.at[1], behind)
    lend_a.start()
    lend_b.start()

    wo_copy.wait()
    eye = jnp.where(
        lax.broadcasted_iota(jnp.int32, (sz.vp, nv), 0) == lax.broadcasted_iota(jnp.int32, (sz.vp, nv), 1), 1.0, 0.0
    ).astype(BF)
    wot[...] = dot(eye, wo_v[...], ((1,), (1,))).astype(BF)

    def edges(i, carry):
        o = lax.rem(i, nx)
        c = lax.div(i, nx)
        at = pl.ds(pl.multiple_of(lax.rem(x + o, nx) * qn + c * CH, CH), CH)
        line = lax.broadcasted_iota(jnp.int32, (ext, CH), 0)
        total = jnp.zeros((ext, CH), F32)
        for k in range(slots.shape[0]):
            used = jnp.where(counts[:, at] > k, coefs[k : k + 1, at].astype(F32), 0.0)
            total = total + jnp.where(line == slots[k : k + 1, at], used, 0.0)
        st[c, :, pl.ds(pl.multiple_of(o * CH, CH), CH)] = total.astype(BF)
        return carry

    lax.fori_loop(0, nc * nx, edges, 0)
    q[...] = jnp.zeros_like(q)
    g[...] = jnp.zeros_like(g)

    def gelu_block(c, j):
        i = c * (nx * ml) + j
        m = lax.rem(j, ml)
        o = lax.div(j, ml)
        slot = lax.rem(i, depth)
        pre_copy(i).wait()
        width = min(lat, 512)

        def some(r, carry):
            at = pl.ds(pl.multiple_of(r * 16, 16), 16)
            to = pl.ds(pl.multiple_of(o * CH + r * 16, 16), 16)
            for n in range(0, lat, width):
                v = pbuf[slot, at, n : n + width].astype(F32)
                v2_ = v * v
                t = jnp.tanh(v * (C_GELU + (C_GELU * A_GELU) * v2_))
                half = 0.5 + 0.5 * t
                hidden = v * half
                hid[c, m, to, n : n + width] = hidden.astype(BF)
                slope = half + hidden * (1.0 - half) * (2.0 * C_GELU + (6.0 * C_GELU * A_GELU) * v2_)
                dg[c, m, to, n : n + width] = slope
            return carry

        lax.fori_loop(0, CH // 16, some, 0)

        @pl.when(i + depth < blocks)
        def _():
            pre_copy(i + depth).start()

    count = float(sz.members)

    def crps_rows(c, at, put, n):
        weight = area[:, pl.ds(pl.multiple_of(x * qn + c * CH, CH), CH)] * vweight[at, :]
        vals = [rb[c, o, m, at, :] for o in range(nx) for m in range(ml)]
        tgt = tgt_v[c, at, :]
        pair = [jnp.zeros((n, CH), F32) for _ in vals]
        for a in range(len(vals)):
            for b in range(a + 1, len(vals)):
                sign = jnp.where(vals[a] > vals[b], 1.0, jnp.where(vals[a] < vals[b], -1.0, 0.0))
                pair[a] = pair[a] + sign
                pair[b] = pair[b] - sign
        for a in range(len(vals)):
            direct = jnp.where(vals[a] > tgt, 1.0, jnp.where(vals[a] < tgt, -1.0, 0.0))
            value = weight * (direct * (1.0 / count) - pair[a] * (1.0 / (count * (count - 1))))
            if n < 16:
                value = jnp.concatenate([value, jnp.zeros((16 - n, CH), F32)], axis=0)
            o, m = a // ml, a % ml
            if o == 0:
                dyb[c, 0, m, put, :] = value.astype(BF)
            else:
                dyo[c, o - 1, m, put, :] = value.astype(BF)

    def crps(c):
        own_copy(c).wait()
        tgt_copy(c).wait()
        for o in range(1, nx):
            forward(c, o).wait_recv()

        def some(r, carry):
            at = pl.ds(pl.multiple_of(r * 16, 16), 16)
            crps_rows(c, at, at, 16)
            return carry

        lax.fori_loop(0, sz.vfull // 16, some, 0)
        if nv > sz.vfull:
            crps_rows(c, slice(sz.vfull, nv), slice(sz.vfull, sz.vp), nv - sz.vfull)
        for o in range(1, nx):
            backward(c, o).start()

    tile = min(256, lat)

    def dense(c):
        for o in range(1, nx):
            backward(c, o).wait_recv()
        for m in range(ml):
            dyt = jnp.concatenate([dyb[c, o, m] for o in range(nx)], axis=1)

            def some(n, carry):
                at = pl.ds(pl.multiple_of(n * tile, tile), tile)
                dhid = dot(dyt, wot[:, at], ((0,), (0,)))
                dpre = (dhid * dg[c, m, :, at]).astype(BF)
                q[m, :, at] += dot(st[c], dpre)
                g[:, at] += dot(dyt, hid[c, m, :, at])
                return carry

            lax.fori_loop(0, lat // tile, some, 0)

    has_prev = jnp.where(s > 0, 1.0, 0.0)
    has_next = jnp.where(s < sz.grid - 1, 1.0, 0.0)

    def transpose_ext():
        lend_a.wait_recv()
        lend_b.wait_recv()

        def some(n, carry):
            at = pl.ds(pl.multiple_of(n * 128, 128), 128)
            for m in range(ml):
                table = jnp.concatenate(
                    [
                        lat_v[m, :, at].astype(F32),
                        lent_r[0, m, :, at].astype(F32) * has_prev,
                        lent_r[1, m, :, at].astype(F32) * has_next,
                    ],
                    axis=0,
                )
                turned = table.T.reshape(64 // sz.rpd, 2, sz.rpd, ext)
                for k in range(2):
                    ext_t[k, pl.ds(pl.multiple_of(n * 64, 64), 64), m * ext : (m + 1) * ext] = (
                        turned[:, k].reshape(64, ext).astype(BF)
                    )
            return carry

        lax.fori_loop(0, lat // 128, some, 0)

    def step(c, carry):
        def block(j, inner):
            gelu_block(c, j)
            return inner

        lax.fori_loop(0, nx * ml, block, 0)
        crps(c)

        @pl.when(c == 0)
        def _():
            transpose_ext()

        @pl.when(c > 0)
        def _():
            dense(c - 1)

        return carry

    lax.fori_loop(0, nc, step, 0)
    dense(nc - 1)

    for m in range(ml):
        qb[m * ext : (m + 1) * ext, :] = q[m].astype(BF)
    give_a = [remote(qb.at[pl.ds(m * ext + rows, halo)], back_r.at[0, m], k_s.at[0, m], k_r.at[0, m], behind) for m in range(ml)]
    give_b = [
        remote(qb.at[pl.ds(m * ext + rows + halo, halo)], back_r.at[1, m], k_s.at[1, m], k_r.at[1, m], ahead) for m in range(ml)
    ]
    core_copies = []
    for p, (start, width) in enumerate(sz.parts):
        score[p][...] = dot(ext_t[other], qb[:, start : start + width]).astype(BF)
        copy = remote(score[p], rcore[p], c_s.at[p], c_r.at[p], mate)
        copy.start()
        core_copies.append(copy)
    g_cs[...] = g[:, pl.ds(pl.multiple_of(other * (lat // 2), 128), lat // 2)].astype(BF)
    g_core = remote(g_cs, g_cr, g_s.at[0], g_r.at[0], mate)
    g_core.start()
    for copy in give_a + give_b:
        copy.start()
    for p, (start, width) in enumerate(sz.parts):
        r1[p][...] = dot(ext_t[core], qb[:, start : start + width]).reshape(nx, ny, nz, sz.rpd, width)

    def pick(ref, order, d):
        at = [slice(None)] * len(ref.shape)
        at[order] = d
        return ref[tuple(at)]

    finals = [g_core] + core_copies + give_a + give_b
    stage1 = []
    for p, (start, width) in enumerate(sz.parts):
        core_copies[p].wait_recv()
        r1[p][...] += rcore[p][...].astype(F32).reshape(nx, ny, nz, sz.rpd, width)
        axis = AXIS_ORDERS[p][0]
        mine = []
        for o in range(1, dims[axis]):
            d, to = peer(axis, o)
            s1[p][o - 1] = pick(r1[p], axis, d).reshape(-1, width).astype(BF)
            copy = remote(s1[p].at[o - 1], v1[p].at[o - 1], a_s.at[p, 0, o - 1], a_r.at[p, 0, o - 1], to)
            copy.start()
            mine.append(copy)
        stage1.append(mine)
        finals += mine

    gw = sz.gcol
    g_core.wait_recv()
    gh[...] = g[:, pl.ds(pl.multiple_of(core * (lat // 2), 128), lat // 2)] + g_cr[...].astype(F32)
    g_zs = []
    for o in range(1, nz):
        d, to = peer(2, o)
        gz_s[o - 1] = gh[:, pl.ds(pl.multiple_of(d * gw, 128), gw)].astype(BF)
        copy = remote(gz_s.at[o - 1], gz_r.at[o - 1], g_s.at[o], g_r.at[o], to)
        copy.start()
        g_zs.append(copy)
    base = nz
    finals += g_zs

    wh_copy.wait()

    def latent_grad(m):
        give_a[m].wait_recv()
        give_b[m].wait_recv()
        line = lax.broadcasted_iota(jnp.int32, (rows, halo), 0)
        put_next = jnp.where(line == next_rows[...], has_next, 0.0).astype(BF)
        put_prev = jnp.where(line == prev_rows[...], has_prev, 0.0).astype(BF)
        whole = q[m, :rows, :] + dot(put_next, back_r[0, m]) + dot(put_prev, back_r[1, m])
        gl[m] = dot(whole.astype(BF), wh_v[...], ((1,), (1,)))
        copy = pltpu.make_async_copy(gl.at[m], out_lat.at[m], out_sem.at[m])
        copy.start()
        return copy

    def gather_sum(buf, value, axis, first):
        here = coord[axis]
        buf[here] = value.astype(buf.dtype)
        copies = []
        for o in range(1, dims[axis]):
            _, to = peer(axis, o)
            copy = remote(buf.at[here], buf.at[here], g_s.at[first + o - 1], g_r.at[first + o - 1], to)
            copy.start()
            copies.append(copy)
        return copies

    outs = [latent_grad(0)]

    for copy in g_zs:
        copy.wait_recv()
    part = gh[:, pl.ds(pl.multiple_of(z * gw, 128), gw)]
    for o in range(1, nz):
        part = part + gz_r[o - 1].astype(F32)
    g_ys = gather_sum(gy, part, 1, base)
    base += ny - 1
    finals += g_ys

    def stage(p, n, copies, src, got, dst, send, land):
        width = sz.parts[p][1]
        order = AXIS_ORDERS[p]
        left = sorted(order[n - 1 :])
        here = left.index(order[n - 1])
        value = pick(src[p], here, coord[order[n - 1]])
        for i, copy in enumerate(copies):
            copy.wait_recv()
            value = value + got[p][i].astype(F32).reshape(value.shape)
        dst[p][...] = value
        axis = order[n]
        here = sorted(order[n:]).index(axis)
        mine = []
        for o in range(1, dims[axis]):
            d, to = peer(axis, o)
            if send is None:
                origin = dst[p].at[d]
            else:
                send[p][o - 1] = pick(dst[p], here, d).reshape(-1, width).astype(BF)
                origin = send[p].at[o - 1]
            copy = remote(origin, land[p].at[o - 1], a_s.at[p, n, o - 1], a_r.at[p, n, o - 1], to)
            copy.start()
            mine.append(copy)
        return mine

    stage2 = [stage(p, 1, stage1[p], r1, v1, r2, s2, v2) for p in range(3)]
    for mine in stage2:
        finals += mine

    for m in range(1, ml):
        outs.append(latent_grad(m))

    for copy in g_ys:
        copy.wait_recv()
    part = gy[0].astype(F32)
    for i in range(1, ny):
        part = part + gy[i].astype(F32)
    g_xs = gather_sum(gx, part, 0, base)
    base += nx - 1
    finals += g_xs

    stage3 = [stage(p, 2, stage2[p], r2, v2, r3, None, v3) for p in range(3)]
    for mine in stage3:
        finals += mine

    scale = 1.0 / math.sqrt(sz.total)
    for copy in g_xs:
        copy.wait_recv()
    part = gx[0].astype(F32)
    for i in range(1, nx):
        part = part + gx[i].astype(F32)
    gfin[core, z] = part * scale
    g_as = []
    for o in range(1, nz):
        _, to = peer(2, o)
        copy = remote(gfin.at[core, z], gfin.at[core, z], g_s.at[base + o - 1], g_r.at[base + o - 1], to)
        copy.start()
        g_as.append(copy)
    base += nz - 1
    finals += g_as

    for p, (start, width) in enumerate(sz.parts):
        value = r3[p][coord[AXIS_ORDERS[p][2]]]
        for i, copy in enumerate(stage3[p]):
            copy.wait_recv()
            value = value + v3[p][i]
        out_wh[:, start : start + width] = value * scale

    for copy in g_as:
        copy.wait_recv()
    g_mate = remote(gfin.at[core], gfin.at[core], g_s.at[base], g_r.at[base], mate)
    g_mate.start()
    finals.append(g_mate)
    g_mate.wait_recv()
    out_wo[...] = gfin[...]

    for copy in finals + [lend_a, lend_b]:
        copy.wait_send()
    for c in range(nc):
        for o in range(1, nx):
            forward(c, o).wait_send()
            backward(c, o).wait_send()
    for copy in outs:
        copy.wait()


def shards(mesh, *args):
    predictions, target, area, var_weight, pre_act, latent, w_hidden, w_out = args[:8]
    edge_slot, edge_count, edge_coef, send_next, send_prev = args[8:]
    sz = Sizes(mesh, predictions, pre_act, latent, send_next)
    nx, ny, nz, ml, lat, vp = sz.nx, sz.ny, sz.nz, sz.ml, sz.lat, sz.vp
    nc, ext, rows, halo = sz.nc, sz.ext, sz.rows, sz.halo
    dims = (nx, ny, nz)
    half = lat // 2

    def per_part(make):
        return [make(p, w) for p, (_, w) in enumerate(sz.parts)]

    def left(p, n):
        return [dims[a] for a in sorted(AXIS_ORDERS[p][n:])]

    def rows_of(p, n):
        return math.prod(left(p, n)) * sz.rpd

    scratch = [
        pltpu.VMEM((ml, rows, lat), BF),
        pltpu.VMEM((lat, lat), BF),
        pltpu.VMEM(w_out.shape, BF),
        pltpu.VMEM((nc, sz.nv, CH), F32),
        pltpu.VMEM((nc, nx, ml, sz.nv, CH), F32),
        pltpu.VMEM((nc, nx - 1, ml, vp, CH), BF),
        pltpu.VMEM((nc, nx, ml, vp, CH), BF),
        pltpu.VMEM((4, CH, lat), BF),
        pltpu.VMEM((nc, ml, nx * CH, lat), BF),
        pltpu.VMEM((nc, ml, nx * CH, lat), F32),
        pltpu.VMEM((nc, ext, nx * CH), BF),
        pltpu.VMEM((vp, lat), BF),
        pltpu.VMEM((ml, ext, lat), F32),
        pltpu.VMEM((ml * ext, lat), BF),
        pltpu.VMEM((vp, lat), F32),
        pltpu.VMEM((2, half, ml * ext), BF),
        pltpu.VMEM((2, ml, halo, lat), BF),
        pltpu.VMEM((2, ml, halo, lat), BF),
        pltpu.VMEM((2, ml, halo, lat), BF),
        pltpu.VMEM((ml, rows, lat), F32),
    ]
    scratch += per_part(lambda p, w: pltpu.VMEM((half, w), BF))
    scratch += per_part(lambda p, w: pltpu.VMEM((half, w), BF))
    scratch += per_part(lambda p, w: pltpu.VMEM((nx, ny, nz, sz.rpd, w), F32))
    for n in (1, 2):
        sends = per_part(lambda p, w: pltpu.VMEM((dims[AXIS_ORDERS[p][n - 1]] - 1, rows_of(p, n), w), BF))
        lands = per_part(lambda p, w: pltpu.VMEM((dims[AXIS_ORDERS[p][n - 1]] - 1, rows_of(p, n), w), BF))
        scratch += sends + lands
        scratch += per_part(lambda p, w: pltpu.VMEM((*left(p, n), sz.rpd, w), F32))
    scratch += per_part(lambda p, w: pltpu.VMEM((dims[AXIS_ORDERS[p][2]] - 1, sz.rpd, w), F32))
    scratch += [
        pltpu.VMEM((vp, half), BF),
        pltpu.VMEM((vp, half), BF),
        pltpu.VMEM((vp, half), F32),
        pltpu.VMEM((nz - 1, vp, sz.gcol), BF),
        pltpu.VMEM((nz - 1, vp, sz.gcol), BF),
        pltpu.VMEM((ny, vp, sz.gcol), BF),
        pltpu.VMEM((nx, vp, sz.gcol), BF),
        pltpu.VMEM((2, nz, vp, sz.gcol), F32),
    ]
    dma = pltpu.SemaphoreType.DMA
    steps = 1 + 2 * (nz - 1) + (ny - 1) + (nx - 1) + 1
    longest = max(dims) - 1
    scratch += [
        dma((3,)),
        dma((nc,)),
        dma((4,)),
        dma((nc,)),
        dma((ml,)),
        dma((nc, nx - 1)),
        dma((nc, nx - 1)),
        dma((nc, nx - 1)),
        dma((nc, nx - 1)),
        dma((2,)),
        dma((2,)),
        dma((2, ml)),
        dma((2, ml)),
        dma((3,)),
        dma((3,)),
        dma((3, 3, longest)),
        dma((3, 3, longest)),
        dma((steps,)),
        dma((steps,)),
    ]
    anywhere = pl.BlockSpec(memory_space=pl.ANY)
    vmem = pl.BlockSpec(memory_space=pltpu.VMEM)
    weights = jnp.pad(var_weight, (0, vp - sz.nv))[:, None]
    grad_latent, grad_w_hidden, grad_w_out = pl.pallas_call(
        functools.partial(kernel, sz),
        out_shape=(
            jax.ShapeDtypeStruct((ml, rows, lat), F32),
            jax.ShapeDtypeStruct((sz.rpd, lat), F32),
            jax.ShapeDtypeStruct((2, nz, vp, sz.gcol), F32),
        ),
        in_specs=[anywhere, anywhere, vmem, vmem, anywhere, anywhere, anywhere, anywhere] + [vmem] * 5,
        out_specs=(anywhere, vmem, vmem),
        scratch_shapes=scratch,
        compiler_params=pltpu.CompilerParams(
            collective_id=0, has_side_effects=True, vmem_limit_bytes=60 * 1024 * 1024
        ),
    )(
        predictions,
        target,
        area[None, :],
        weights,
        pre_act,
        latent,
        w_hidden,
        w_out,
        edge_slot.T,
        edge_count[None, :],
        edge_coef.T,
        send_next[None, :],
        send_prev[None, :],
    )
    grad_w_out = jnp.swapaxes(grad_w_out, 2, 3).reshape(lat, vp)[:, : sz.nv]
    return (grad_latent, grad_w_hidden, grad_w_out)


def solution(mesh):
    in_specs = (
        P("member", None, "grid"),
        P(None, "grid"),
        P("grid"),
        P(),
        P("member", "grid", None),
        P("member", "grid", None),
        P(),
        P(),
        P("grid", None),
        P("grid"),
        P("grid", None),
        P("grid"),
        P("grid"),
    )
    out_specs = (P("member", "grid", None), P(("member", "grid"), None), P())
    return jax.shard_map(
        functools.partial(shards, mesh), mesh=mesh, in_specs=in_specs, out_specs=out_specs, check_vma=False
    )
```

```python
import functools
import math

import jax
import jax.numpy as jnp
from jax import lax
from jax.experimental import pallas as pl
from jax.experimental.pallas import tpu as pltpu
from jax.sharding import PartitionSpec as P

MESH_ID = pl.DeviceIdType.MESH
C_GELU = math.sqrt(2.0 / math.pi)
A_GELU = 0.044715
CH = 128
PRE_SLOTS = 8
BF = jnp.bfloat16
F32 = jnp.float32


def column_parts(lat):
    tiles = lat // 128
    sizes = [tiles // 3 + (1 if i < tiles % 3 else 0) for i in range(3)]
    parts, start = [], 0
    for size in sizes:
        parts.append((start * 128, size * 128))
        start += size
    return parts


def dot(a, b, dims=((1,), (0,))):
    return lax.dot_general(a, b, (dims, ((), ())), preferred_element_type=F32)


class Sizes:
    def __init__(self, mesh, predictions, pre_act, latent, send_next):
        self.nx = mesh.shape["member"]
        self.grid = mesh.shape["grid"]
        chips = self.grid // 2
        self.ny = math.isqrt(chips)
        self.nz = chips // self.ny
        self.nv, self.ml, self.npts = predictions.shape
        self.lat = pre_act.shape[2]
        self.rows = latent.shape[1]
        self.halo = send_next.shape[0]
        self.ext = self.rows + 2 * self.halo
        self.qn = self.npts // self.nx
        self.nc = self.qn // CH
        self.vfull = self.nv // 16 * 16
        self.vp = -(-self.nv // 16) * 16
        self.rpd = self.lat // (self.nx * self.grid)
        self.members = self.nx * self.ml
        self.gcol = self.lat // 2 // self.nz
        self.parts = column_parts(self.lat)
        self.total = self.members * self.npts * self.grid


AXIS_ORDERS = ((2, 1, 0), (1, 0, 2), (0, 2, 1))


def kernel(sz, *refs):
    it = iter(refs)
    preds, target, area, vweight, pre, latent, w_hidden, w_out = [next(it) for _ in range(8)]
    slots, counts, coefs, next_rows, prev_rows = [next(it) for _ in range(5)]
    out_lat, out_wh, out_wo = [next(it) for _ in range(3)]
    lat_v, wh_v, wo_v, tgt_v = [next(it) for _ in range(4)]
    rb, dyo, dyb, pbuf, hid, dg, st, wot, vcol = [next(it) for _ in range(9)]
    q, qb, g, ext_t = [next(it) for _ in range(4)]
    lent_s, lent_r, back_r, gl = [next(it) for _ in range(4)]
    score = [next(it) for _ in range(3)]
    rcore = [next(it) for _ in range(3)]
    r1 = [next(it) for _ in range(3)]
    s1 = [next(it) for _ in range(3)]
    v1 = [next(it) for _ in range(3)]
    r2 = [next(it) for _ in range(3)]
    s2 = [next(it) for _ in range(3)]
    v2 = [next(it) for _ in range(3)]
    r3 = [next(it) for _ in range(3)]
    v3 = [next(it) for _ in range(3)]
    g_cs, g_cr, gh, gz_s, gz_r, gy, gx, gfin = [next(it) for _ in range(8)]
    loc_sem, own_sem, pre_sem, tgt_sem, out_sem = [next(it) for _ in range(5)]
    f_s, f_r, b_s, b_r, h_s, h_r, k_s, k_r = [next(it) for _ in range(8)]
    c_s, c_r, a_s, a_r, g_s, g_r = [next(it) for _ in range(6)]

    nx, ny, nz, ml, nv, lat = sz.nx, sz.ny, sz.nz, sz.ml, sz.nv, sz.lat
    nc, qn, ext, rows, halo = sz.nc, sz.qn, sz.ext, sz.rows, sz.halo
    dims = (nx, ny, nz)
    x = lax.axis_index("member")
    s = lax.axis_index("grid")
    core = lax.rem(s, 2)
    z = lax.rem(lax.div(s, 2), nz)
    y = lax.div(s, 2 * nz)
    other = 1 - core
    coord = (x, y, z)

    def device(cx, cy, cz, cc):
        return (cx, (cy * nz + cz) * 2 + cc)

    def peer(axis, by):
        there = list(coord)
        there[axis] = lax.rem(coord[axis] + by, dims[axis])
        return there[axis], device(*there, core)

    mate = device(x, y, z, other)
    behind = (x, lax.rem(s + sz.grid - 1, sz.grid))
    ahead = (x, lax.rem(s + 1, sz.grid))

    def remote(src, dst, send_sem, recv_sem, to):
        return pltpu.make_async_remote_copy(
            src_ref=src, dst_ref=dst, send_sem=send_sem, recv_sem=recv_sem, device_id=to, device_id_type=MESH_ID
        )

    def own_copy(c):
        return pltpu.make_async_copy(
            preds.at[:, :, pl.ds(pl.multiple_of(x * qn + c * CH, CH), CH)], rb.at[c, 0], own_sem.at[c]
        )

    def tgt_copy(c):
        return pltpu.make_async_copy(
            target.at[:, pl.ds(pl.multiple_of(x * qn + c * CH, CH), CH)], tgt_v.at[c], tgt_sem.at[c]
        )

    def forward(c, o):
        there, to = peer(0, o)
        return remote(
            preds.at[:, :, pl.ds(pl.multiple_of(there * qn + c * CH, CH), CH)],
            rb.at[c, o],
            f_s.at[c, o - 1],
            f_r.at[c, o - 1],
            to,
        )

    def backward(c, o):
        _, to = peer(0, nx - o)
        return remote(dyo.at[c, o - 1], dyb.at[c, o], b_s.at[c, o - 1], b_r.at[c, o - 1], to)

    blocks = nc * nx * ml
    depth = pbuf.shape[0]

    def pre_copy(i):
        m = lax.rem(i, ml)
        o = lax.rem(lax.div(i, ml), nx)
        c = lax.div(i, ml * nx)
        quarter = lax.rem(x + o, nx)
        slot = lax.rem(i, depth)
        return pltpu.make_async_copy(
            pre.at[m, pl.ds(pl.multiple_of(quarter * qn + c * CH, CH), CH), :], pbuf.at[slot], pre_sem.at[slot]
        )

    lat_copy = pltpu.make_async_copy(latent, lat_v, loc_sem.at[0])
    wo_copy = pltpu.make_async_copy(w_out, wo_v, loc_sem.at[1])
    wh_copy = pltpu.make_async_copy(w_hidden, wh_v, loc_sem.at[2])

    lat_copy.start()
    for i in range(depth):
        pre_copy(i).start()

    wo_copy.start()
    barrier = pltpu.get_barrier_semaphore()
    neighbours = [peer(a, o)[1] for a in range(3) for o in range(1, dims[a])] + [behind, ahead]
    for to in neighbours:
        pl.semaphore_signal(barrier, inc=1, device_id=to, device_id_type=MESH_ID)

    wo_copy.wait()
    wot[: sz.vfull] = wo_v[: sz.vfull]
    if sz.vp > sz.vfull:
        rest = jnp.concatenate(
            [wo_v[sz.vfull : nv].astype(F32), jnp.zeros((sz.vp - nv, lat), F32)], axis=0
        )
        wot[sz.vfull :] = rest.astype(BF)
    shape = (sz.vp, nv)
    same = lax.broadcasted_iota(jnp.int32, shape, 0) == lax.broadcasted_iota(jnp.int32, shape, 1)
    column = jnp.sum(jnp.where(same, vweight[...], 0.0), axis=1, keepdims=True)
    vcol[...] = jnp.broadcast_to(column, vcol.shape)

    def edges(i, carry):
        o = lax.rem(i, nx)
        c = lax.div(i, nx)
        at = pl.ds(pl.multiple_of(lax.rem(x + o, nx) * qn + c * CH, CH), CH)
        line = lax.broadcasted_iota(jnp.int32, (ext, CH), 0)
        total = jnp.zeros((ext, CH), F32)
        for k in range(slots.shape[0]):
            used = jnp.where(counts[:, at] > k, coefs[k : k + 1, at].astype(F32), 0.0)
            total = total + jnp.where(line == slots[k : k + 1, at], used, 0.0)
        st[c, :, pl.ds(pl.multiple_of(o * CH, CH), CH)] = total.astype(BF)
        return carry

    lax.fori_loop(0, nc * nx, edges, 0)
    q[...] = jnp.zeros_like(q)
    g[...] = jnp.zeros_like(g)

    pl.semaphore_wait(barrier, len(neighbours))

    for c in range(nc):
        for o in range(1, nx):
            forward(c, o).start()
        own_copy(c).start()
        tgt_copy(c).start()
    wh_copy.start()

    lat_copy.wait()
    line = lax.broadcasted_iota(jnp.int32, (rows, halo), 0)
    pick_next = jnp.where(line == next_rows[...], 1.0, 0.0).astype(BF)
    pick_prev = jnp.where(line == prev_rows[...], 1.0, 0.0).astype(BF)
    for m in range(ml):
        lent_s[0, m] = dot(pick_next, lat_v[m], ((0,), (0,))).astype(BF)
        lent_s[1, m] = dot(pick_prev, lat_v[m], ((0,), (0,))).astype(BF)
    lend_a = remote(lent_s.at[0], lent_r.at[0], h_s.at[0], h_r.at[0], ahead)
    lend_b = remote(lent_s.at[1], lent_r.at[1], h_s.at[1], h_r.at[1], behind)
    lend_a.start()
    lend_b.start()

    def gelu_block(i):
        m = lax.rem(i, ml)
        o = lax.rem(lax.div(i, ml), nx)
        c = lax.div(i, ml * nx)
        slot = lax.rem(i, depth)
        pre_copy(i).wait()
        width = min(lat, 512)

        def some(r, carry):
            at = pl.ds(pl.multiple_of(r * 16, 16), 16)
            to = pl.ds(pl.multiple_of(o * CH + r * 16, 16), 16)
            for n in range(0, lat, width):
                v = pbuf[slot, at, n : n + width].astype(F32)
                v2_ = v * v
                t = jnp.tanh(v * (C_GELU + (C_GELU * A_GELU) * v2_))
                half = 0.5 + 0.5 * t
                hidden = v * half
                hid[c, m, to, n : n + width] = hidden.astype(BF)
                slope = half + hidden * (1.0 - half) * (2.0 * C_GELU + (6.0 * C_GELU * A_GELU) * v2_)
                dg[c, m, to, n : n + width] = slope
            return carry

        lax.fori_loop(0, CH // 16, some, 0)

        @pl.when(i + depth < blocks)
        def _():
            pre_copy(i + depth).start()

    count = float(sz.members)

    def crps_rows(c, at, put, n):
        weight = area[:, pl.ds(pl.multiple_of(x * qn + c * CH, CH), CH)] * vcol[at, :]
        vals = [rb[c, o, at, m, :] for o in range(nx) for m in range(ml)]
        tgt = tgt_v[c, at, :]
        pair = [jnp.zeros((n, CH), F32) for _ in vals]
        for a in range(len(vals)):
            for b in range(a + 1, len(vals)):
                sign = jnp.where(vals[a] > vals[b], 1.0, jnp.where(vals[a] < vals[b], -1.0, 0.0))
                pair[a] = pair[a] + sign
                pair[b] = pair[b] - sign
        for a in range(len(vals)):
            direct = jnp.where(vals[a] > tgt, 1.0, jnp.where(vals[a] < tgt, -1.0, 0.0))
            value = weight * (direct * (1.0 / count) - pair[a] * (1.0 / (count * (count - 1))))
            if n < 16:
                value = jnp.concatenate([value, jnp.zeros((16 - n, CH), F32)], axis=0)
            o, m = a // ml, a % ml
            if o == 0:
                dyb[c, 0, m, put, :] = value.astype(BF)
            else:
                dyo[c, o - 1, m, put, :] = value.astype(BF)

    def crps(c):
        own_copy(c).wait()
        tgt_copy(c).wait()
        for o in range(1, nx):
            forward(c, o).wait_recv()

        def some(r, carry):
            at = pl.ds(pl.multiple_of(r * 16, 16), 16)
            crps_rows(c, at, at, 16)
            return carry

        lax.fori_loop(0, sz.vfull // 16, some, 0)
        if nv > sz.vfull:
            crps_rows(c, slice(sz.vfull, nv), slice(sz.vfull, sz.vp), nv - sz.vfull)
        for o in range(1, nx):
            backward(c, o).start()

    g_core = remote(g_cs, g_cr, g_s.at[0], g_r.at[0], mate)

    def dense(c):
        for o in range(1, nx):
            backward(c, o).wait_recv()
        dyt = [jnp.concatenate([dyb[c, o, m] for o in range(nx)], axis=1) for m in range(ml)]
        for m in range(ml):
            g[...] += dot(dyt[m], hid[c, m])

        @pl.when(c == nc - 1)
        def _():
            g_cs[...] = g[:, pl.ds(pl.multiple_of(other * (lat // 2), 128), lat // 2)].astype(BF)
            g_core.start()

        for m in range(ml):
            dpre = (dot(dyt[m], wot[...], ((0,), (0,))) * dg[c, m]).astype(BF)
            q[m] += dot(st[c], dpre)

    has_prev = jnp.where(s > 0, 1.0, 0.0)
    has_next = jnp.where(s < sz.grid - 1, 1.0, 0.0)

    def transpose_ext():
        lend_a.wait_recv()
        lend_b.wait_recv()

        def some(n, carry):
            at = pl.ds(pl.multiple_of(n * 128, 128), 128)
            for m in range(ml):
                table = jnp.concatenate(
                    [
                        lat_v[m, :, at].astype(F32),
                        lent_r[0, m, :, at].astype(F32) * has_prev,
                        lent_r[1, m, :, at].astype(F32) * has_next,
                    ],
                    axis=0,
                )
                turned = table.T.reshape(64 // sz.rpd, 2, sz.rpd, ext)
                for k in range(2):
                    ext_t[k, pl.ds(pl.multiple_of(n * 64, 64), 64), m * ext : (m + 1) * ext] = (
                        turned[:, k].reshape(64, ext).astype(BF)
                    )
            return carry

        lax.fori_loop(0, lat // 128, some, 0)

    def each(last, body):
        def one(i, carry):
            body(i)
            return carry

        lax.fori_loop(0, last, one, 0)

    each(blocks, gelu_block)
    transpose_ext()
    each(nc, crps)
    each(nc, dense)

    for m in range(ml):
        qb[m * ext : (m + 1) * ext, :] = q[m].astype(BF)
    give_a = [remote(qb.at[pl.ds(m * ext + rows, halo)], back_r.at[0, m], k_s.at[0, m], k_r.at[0, m], behind) for m in range(ml)]
    give_b = [
        remote(qb.at[pl.ds(m * ext + rows + halo, halo)], back_r.at[1, m], k_s.at[1, m], k_r.at[1, m], ahead) for m in range(ml)
    ]
    for copy in give_a + give_b:
        copy.start()
    core_copies = []
    for p, (start, width) in enumerate(sz.parts):
        score[p][...] = dot(ext_t[other], qb[:, start : start + width]).astype(BF)
        copy = remote(score[p], rcore[p], c_s.at[p], c_r.at[p], mate)
        copy.start()
        core_copies.append(copy)
    finals = [g_core] + core_copies + give_a + give_b

    def pick(ref, order, d):
        at = [slice(None)] * len(ref.shape)
        at[order] = d
        return ref[tuple(at)]

    gw = sz.gcol
    g_core.wait_recv()
    gh[...] = g[:, pl.ds(pl.multiple_of(core * (lat // 2), 128), lat // 2)] + g_cr[...].astype(F32)
    g_zs = []
    for o in range(1, nz):
        d, to = peer(2, o)
        gz_s[o - 1] = gh[:, pl.ds(pl.multiple_of(d * gw, 128), gw)].astype(BF)
        copy = remote(gz_s.at[o - 1], gz_r.at[o - 1], g_s.at[o], g_r.at[o], to)
        copy.start()
        g_zs.append(copy)
    base = nz
    finals += g_zs

    for p, (start, width) in enumerate(sz.parts):
        r1[p][...] = dot(ext_t[core], qb[:, start : start + width]).reshape(nx, ny, nz, sz.rpd, width)

    def gather_sum(buf, value, axis, first):
        here = coord[axis]
        buf[here] = value.astype(buf.dtype)
        copies = []
        for o in range(1, dims[axis]):
            _, to = peer(axis, o)
            copy = remote(buf.at[here], buf.at[here], g_s.at[first + o - 1], g_r.at[first + o - 1], to)
            copy.start()
            copies.append(copy)
        return copies

    def gathered(buf, copies):
        for copy in copies:
            copy.wait_recv()
        part = buf[0].astype(F32)
        for i in range(1, buf.shape[0]):
            part = part + buf[i].astype(F32)
        return part

    for copy in g_zs:
        copy.wait_recv()
    part = gh[:, pl.ds(pl.multiple_of(z * gw, 128), gw)]
    for o in range(1, nz):
        part = part + gz_r[o - 1].astype(F32)
    g_ys = gather_sum(gy, part, 1, base)
    base += ny - 1
    finals += g_ys

    stage1 = []
    for p, (start, width) in enumerate(sz.parts):
        core_copies[p].wait_recv()
        r1[p][...] += rcore[p][...].astype(F32).reshape(nx, ny, nz, sz.rpd, width)
        axis = AXIS_ORDERS[p][0]
        mine = []
        for o in range(1, dims[axis]):
            d, to = peer(axis, o)
            s1[p][o - 1] = pick(r1[p], axis, d).reshape(-1, width).astype(BF)
            copy = remote(s1[p].at[o - 1], v1[p].at[o - 1], a_s.at[p, 0, o - 1], a_r.at[p, 0, o - 1], to)
            copy.start()
            mine.append(copy)
        stage1.append(mine)
        finals += mine

    g_xs = gather_sum(gx, gathered(gy, g_ys), 0, base)
    base += nx - 1
    finals += g_xs

    wh_copy.wait()

    def latent_grad(m):
        give_a[m].wait_recv()
        give_b[m].wait_recv()
        line = lax.broadcasted_iota(jnp.int32, (rows, halo), 0)
        put_next = jnp.where(line == next_rows[...], has_next, 0.0).astype(BF)
        put_prev = jnp.where(line == prev_rows[...], has_prev, 0.0).astype(BF)
        whole = q[m, :rows, :] + dot(put_next, back_r[0, m]) + dot(put_prev, back_r[1, m])
        gl[m] = dot(whole.astype(BF), wh_v[...], ((1,), (1,)))
        copy = pltpu.make_async_copy(gl.at[m], out_lat.at[m], out_sem.at[m])
        copy.start()
        return copy

    outs = [latent_grad(0)]

    def stage(p, n, copies, src, got, dst, send, land):
        width = sz.parts[p][1]
        order = AXIS_ORDERS[p]
        left = sorted(order[n - 1 :])
        here = left.index(order[n - 1])
        value = pick(src[p], here, coord[order[n - 1]])
        for i, copy in enumerate(copies):
            copy.wait_recv()
            value = value + got[p][i].astype(F32).reshape(value.shape)
        dst[p][...] = value
        axis = order[n]
        here = sorted(order[n:]).index(axis)
        mine = []
        for o in range(1, dims[axis]):
            d, to = peer(axis, o)
            if send is None:
                origin = dst[p].at[d]
            else:
                send[p][o - 1] = pick(dst[p], here, d).reshape(-1, width).astype(BF)
                origin = send[p].at[o - 1]
            copy = remote(origin, land[p].at[o - 1], a_s.at[p, n, o - 1], a_r.at[p, n, o - 1], to)
            copy.start()
            mine.append(copy)
        return mine

    stage2 = [stage(p, 1, stage1[p], r1, v1, r2, s2, v2) for p in range(3)]
    for mine in stage2:
        finals += mine

    scale = 1.0 / math.sqrt(sz.total)
    gfin[core, z] = gathered(gx, g_xs) * scale
    g_as = []
    for o in range(1, nz):
        _, to = peer(2, o)
        copy = remote(gfin.at[core, z], gfin.at[core, z], g_s.at[base + o - 1], g_r.at[base + o - 1], to)
        copy.start()
        g_as.append(copy)
    base += nz - 1
    finals += g_as

    for m in range(1, ml):
        outs.append(latent_grad(m))

    stage3 = [stage(p, 2, stage2[p], r2, v2, r3, None, v3) for p in range(3)]
    for mine in stage3:
        finals += mine

    for copy in g_as:
        copy.wait_recv()
    g_mate = remote(gfin.at[core], gfin.at[core], g_s.at[base], g_r.at[base], mate)
    g_mate.start()
    finals.append(g_mate)

    for p, (start, width) in enumerate(sz.parts):
        value = r3[p][coord[AXIS_ORDERS[p][2]]]
        for i, copy in enumerate(stage3[p]):
            copy.wait_recv()
            value = value + v3[p][i]
        out_wh[:, start : start + width] = value * scale

    g_mate.wait_recv()
    for k in range(2):
        for i in range(nz):
            at = (k * nz + i) * gw
            out_wo[:, at : at + gw] = gfin[k, i, :nv, :]

    for copy in finals + [lend_a, lend_b]:
        copy.wait_send()
    for c in range(nc):
        for o in range(1, nx):
            forward(c, o).wait_send()
            backward(c, o).wait_send()
    for copy in outs:
        copy.wait()


def shards(mesh, *args):
    predictions, target, area, var_weight, pre_act, latent, w_hidden, w_out = args[:8]
    predictions = jnp.swapaxes(predictions, 0, 1)
    w_out = w_out.T
    edge_slot, edge_count, edge_coef, send_next, send_prev = args[8:]
    sz = Sizes(mesh, predictions, pre_act, latent, send_next)
    nx, ny, nz, ml, lat, vp = sz.nx, sz.ny, sz.nz, sz.ml, sz.lat, sz.vp
    nc, ext, rows, halo = sz.nc, sz.ext, sz.rows, sz.halo
    dims = (nx, ny, nz)
    half = lat // 2

    def per_part(make):
        return [make(p, w) for p, (_, w) in enumerate(sz.parts)]

    def left(p, n):
        return [dims[a] for a in sorted(AXIS_ORDERS[p][n:])]

    def rows_of(p, n):
        return math.prod(left(p, n)) * sz.rpd

    scratch = [
        pltpu.VMEM((ml, rows, lat), BF),
        pltpu.VMEM((lat, lat), BF),
        pltpu.VMEM(w_out.shape, BF),
        pltpu.VMEM((nc, sz.nv, CH), F32),
        pltpu.VMEM((nc, nx, sz.nv, ml, CH), F32),
        pltpu.VMEM((nc, nx - 1, ml, vp, CH), BF),
        pltpu.VMEM((nc, nx, ml, vp, CH), BF),
        pltpu.VMEM((PRE_SLOTS, CH, lat), BF),
        pltpu.VMEM((nc, ml, nx * CH, lat), BF),
        pltpu.VMEM((nc, ml, nx * CH, lat), F32),
        pltpu.VMEM((nc, ext, nx * CH), BF),
        pltpu.VMEM((vp, lat), BF),
        pltpu.VMEM((vp, CH), F32),
        pltpu.VMEM((ml, ext, lat), F32),
        pltpu.VMEM((ml * ext, lat), BF),
        pltpu.VMEM((vp, lat), F32),
        pltpu.VMEM((2, half, ml * ext), BF),
        pltpu.VMEM((2, ml, halo, lat), BF),
        pltpu.VMEM((2, ml, halo, lat), BF),
        pltpu.VMEM((2, ml, halo, lat), BF),
        pltpu.VMEM((ml, rows, lat), F32),
    ]
    scratch += per_part(lambda p, w: pltpu.VMEM((half, w), BF))
    scratch += per_part(lambda p, w: pltpu.VMEM((half, w), BF))
    scratch += per_part(lambda p, w: pltpu.VMEM((nx, ny, nz, sz.rpd, w), F32))
    for n in (1, 2):
        sends = per_part(lambda p, w: pltpu.VMEM((dims[AXIS_ORDERS[p][n - 1]] - 1, rows_of(p, n), w), BF))
        lands = per_part(lambda p, w: pltpu.VMEM((dims[AXIS_ORDERS[p][n - 1]] - 1, rows_of(p, n), w), BF))
        scratch += sends + lands
        scratch += per_part(lambda p, w: pltpu.VMEM((*left(p, n), sz.rpd, w), F32))
    scratch += per_part(lambda p, w: pltpu.VMEM((dims[AXIS_ORDERS[p][2]] - 1, sz.rpd, w), F32))
    scratch += [
        pltpu.VMEM((vp, half), BF),
        pltpu.VMEM((vp, half), BF),
        pltpu.VMEM((vp, half), F32),
        pltpu.VMEM((nz - 1, vp, sz.gcol), BF),
        pltpu.VMEM((nz - 1, vp, sz.gcol), BF),
        pltpu.VMEM((ny, vp, sz.gcol), BF),
        pltpu.VMEM((nx, vp, sz.gcol), BF),
        pltpu.VMEM((2, nz, vp, sz.gcol), F32),
    ]
    dma = pltpu.SemaphoreType.DMA
    steps = 1 + 2 * (nz - 1) + (ny - 1) + (nx - 1) + 1
    longest = max(dims) - 1
    scratch += [
        dma((3,)),
        dma((nc,)),
        dma((PRE_SLOTS,)),
        dma((nc,)),
        dma((ml,)),
        dma((nc, nx - 1)),
        dma((nc, nx - 1)),
        dma((nc, nx - 1)),
        dma((nc, nx - 1)),
        dma((2,)),
        dma((2,)),
        dma((2, ml)),
        dma((2, ml)),
        dma((3,)),
        dma((3,)),
        dma((3, 3, longest)),
        dma((3, 3, longest)),
        dma((steps,)),
        dma((steps,)),
    ]
    anywhere = pl.BlockSpec(memory_space=pl.ANY)
    vmem = pl.BlockSpec(memory_space=pltpu.VMEM)
    grad_latent, grad_w_hidden, grad_w_out = pl.pallas_call(
        functools.partial(kernel, sz),
        out_shape=(
            jax.ShapeDtypeStruct((ml, rows, lat), F32),
            jax.ShapeDtypeStruct((sz.rpd, lat), F32),
            jax.ShapeDtypeStruct((sz.nv, lat), F32),
        ),
        in_specs=[anywhere, anywhere, vmem, vmem, anywhere, anywhere, anywhere, anywhere] + [vmem] * 5,
        out_specs=(anywhere, vmem, vmem),
        scratch_shapes=scratch,
        compiler_params=pltpu.CompilerParams(
            collective_id=0, has_side_effects=True, vmem_limit_bytes=60 * 1024 * 1024
        ),
    )(
        predictions,
        target,
        area[None, :],
        var_weight[None, :],
        pre_act,
        latent,
        w_hidden,
        w_out,
        edge_slot.T,
        edge_count[None, :],
        edge_coef.T,
        send_next[None, :],
        send_prev[None, :],
    )
    return (grad_latent, grad_w_hidden, grad_w_out.T)


def solution(mesh):
    in_specs = (
        P("member", None, "grid"),
        P(None, "grid"),
        P("grid"),
        P(),
        P("member", "grid", None),
        P("member", "grid", None),
        P(),
        P(),
        P("grid", None),
        P("grid"),
        P("grid", None),
        P("grid"),
        P("grid"),
    )
    out_specs = (P("member", "grid", None), P(("member", "grid"), None), P())
    return jax.shard_map(
        functools.partial(shards, mesh), mesh=mesh, in_specs=in_specs, out_specs=out_specs, check_vma=False
    )
```

```python
import functools
import math

import jax
import jax.numpy as jnp
from jax import lax
from jax.experimental import pallas as pl
from jax.experimental.pallas import tpu as pltpu
from jax.sharding import PartitionSpec as P

MESH_ID = pl.DeviceIdType.MESH
C_GELU = math.sqrt(2.0 / math.pi)
A_GELU = 0.044715
CH = 128
PRE_SLOTS = 8
BF = jnp.bfloat16
F32 = jnp.float32


def column_parts(lat):
    tiles = lat // 128
    sizes = [tiles // 3 + (1 if i < tiles % 3 else 0) for i in range(3)]
    parts, start = [], 0
    for size in sizes:
        parts.append((start * 128, size * 128))
        start += size
    return parts


def dot(a, b, dims=((1,), (0,))):
    return lax.dot_general(a, b, (dims, ((), ())), preferred_element_type=F32)


class Sizes:
    def __init__(self, mesh, predictions, pre_act, latent, send_next):
        self.nx = mesh.shape["member"]
        self.grid = mesh.shape["grid"]
        chips = self.grid // 2
        self.ny = math.isqrt(chips)
        self.nz = chips // self.ny
        self.nv, self.ml, self.npts = predictions.shape
        self.lat = pre_act.shape[2]
        self.rows = latent.shape[1]
        self.halo = send_next.shape[0]
        self.ext = self.rows + 2 * self.halo
        self.qn = self.npts // self.nx
        self.nc = self.qn // CH
        self.vfull = self.nv // 16 * 16
        self.vp = -(-self.nv // 16) * 16
        self.rpd = self.lat // (self.nx * self.grid)
        self.members = self.nx * self.ml
        self.gcol = self.lat // 2 // self.nz
        self.parts = column_parts(self.lat)
        self.total = self.members * self.npts * self.grid


AXIS_ORDERS = ((2, 1, 0), (1, 0, 2), (0, 2, 1))


def kernel(sz, *refs):
    it = iter(refs)
    preds, target, area, vweight, pre, latent, w_hidden, w_out = [next(it) for _ in range(8)]
    slots, counts, coefs, next_rows, prev_rows = [next(it) for _ in range(5)]
    out_lat, out_wh, out_wo = [next(it) for _ in range(3)]
    lat_v, wh_v, wo_v, tgt_v = [next(it) for _ in range(4)]
    rb, dyo, dyb, pbuf, hid, dg, st, wot, vcol = [next(it) for _ in range(9)]
    q, qb, g, ext_t = [next(it) for _ in range(4)]
    lent_s, lent_r, back_r, gl = [next(it) for _ in range(4)]
    score = [next(it) for _ in range(3)]
    rcore = [next(it) for _ in range(3)]
    r1 = [next(it) for _ in range(3)]
    s1 = [next(it) for _ in range(3)]
    v1 = [next(it) for _ in range(3)]
    r2 = [next(it) for _ in range(3)]
    s2 = [next(it) for _ in range(3)]
    v2 = [next(it) for _ in range(3)]
    r3 = [next(it) for _ in range(3)]
    v3 = [next(it) for _ in range(3)]
    ga_s, ga_r, gy, gx, gfin = [next(it) for _ in range(5)]
    loc_sem, own_sem, pre_sem, tgt_sem, out_sem = [next(it) for _ in range(5)]
    f_s, f_r, b_s, b_r, h_s, h_r, k_s, k_r = [next(it) for _ in range(8)]
    c_s, c_r, a_s, a_r, g_s, g_r = [next(it) for _ in range(6)]

    nx, ny, nz, ml, nv, lat = sz.nx, sz.ny, sz.nz, sz.ml, sz.nv, sz.lat
    nc, qn, ext, rows, halo = sz.nc, sz.qn, sz.ext, sz.rows, sz.halo
    dims = (nx, ny, nz)
    x = lax.axis_index("member")
    s = lax.axis_index("grid")
    core = lax.rem(s, 2)
    z = lax.rem(lax.div(s, 2), nz)
    y = lax.div(s, 2 * nz)
    other = 1 - core
    coord = (x, y, z)

    def device(cx, cy, cz, cc):
        return (cx, (cy * nz + cz) * 2 + cc)

    def peer(axis, by):
        there = list(coord)
        there[axis] = lax.rem(coord[axis] + by, dims[axis])
        return there[axis], device(*there, core)

    mate = device(x, y, z, other)
    group = []
    for by in range(nz):
        for swap in range(2):
            if by + swap > 0:
                there, kept = lax.rem(z + by, nz), other if swap else core
                group.append((there, kept, device(x, y, there, kept)))
    behind = (x, lax.rem(s + sz.grid - 1, sz.grid))
    ahead = (x, lax.rem(s + 1, sz.grid))

    def remote(src, dst, send_sem, recv_sem, to):
        return pltpu.make_async_remote_copy(
            src_ref=src, dst_ref=dst, send_sem=send_sem, recv_sem=recv_sem, device_id=to, device_id_type=MESH_ID
        )

    def own_copy(c):
        return pltpu.make_async_copy(
            preds.at[:, :, pl.ds(pl.multiple_of(x * qn + c * CH, CH), CH)], rb.at[c, 0], own_sem.at[c]
        )

    def tgt_copy(c):
        return pltpu.make_async_copy(
            target.at[:, pl.ds(pl.multiple_of(x * qn + c * CH, CH), CH)], tgt_v.at[c], tgt_sem.at[c]
        )

    def forward(c, o):
        there, to = peer(0, o)
        return remote(
            preds.at[:, :, pl.ds(pl.multiple_of(there * qn + c * CH, CH), CH)],
            rb.at[c, o],
            f_s.at[c, o - 1],
            f_r.at[c, o - 1],
            to,
        )

    def backward(c, o):
        _, to = peer(0, nx - o)
        return remote(dyo.at[c, o - 1], dyb.at[c, o], b_s.at[c, o - 1], b_r.at[c, o - 1], to)

    blocks = nc * nx * ml
    depth = pbuf.shape[0]

    def pre_copy(i):
        m = lax.rem(i, ml)
        o = lax.rem(lax.div(i, ml), nx)
        c = lax.div(i, ml * nx)
        quarter = lax.rem(x + o, nx)
        slot = lax.rem(i, depth)
        return pltpu.make_async_copy(
            pre.at[m, pl.ds(pl.multiple_of(quarter * qn + c * CH, CH), CH), :], pbuf.at[slot], pre_sem.at[slot]
        )

    lat_copy = pltpu.make_async_copy(latent, lat_v, loc_sem.at[0])
    wo_copy = pltpu.make_async_copy(w_out, wo_v, loc_sem.at[1])
    wh_copy = pltpu.make_async_copy(w_hidden, wh_v, loc_sem.at[2])

    lat_copy.start()
    for i in range(depth):
        pre_copy(i).start()

    wo_copy.start()
    barrier = pltpu.get_barrier_semaphore()
    neighbours = [peer(a, o)[1] for a in range(2) for o in range(1, dims[a])] + [behind, ahead]
    neighbours += [to for _, _, to in group]
    for to in neighbours:
        pl.semaphore_signal(barrier, inc=1, device_id=to, device_id_type=MESH_ID)

    pl.semaphore_wait(barrier, len(neighbours))

    for c in range(nc):
        if c < 1:
            for o in range(1, nx):
                forward(c, o).start()
        own_copy(c).start()
        tgt_copy(c).start()
    wh_copy.start()

    lat_copy.wait()
    line = lax.broadcasted_iota(jnp.int32, (rows, halo), 0)
    pick_next = jnp.where(line == next_rows[...], 1.0, 0.0).astype(BF)
    pick_prev = jnp.where(line == prev_rows[...], 1.0, 0.0).astype(BF)
    for m in range(ml):
        lent_s[0, m] = dot(pick_next, lat_v[m], ((0,), (0,))).astype(BF)
        lent_s[1, m] = dot(pick_prev, lat_v[m], ((0,), (0,))).astype(BF)
    lend_a = remote(lent_s.at[0], lent_r.at[0], h_s.at[0], h_r.at[0], ahead)
    lend_b = remote(lent_s.at[1], lent_r.at[1], h_s.at[1], h_r.at[1], behind)
    lend_a.start()
    lend_b.start()

    wo_copy.wait()
    wot[: sz.vfull] = wo_v[: sz.vfull]
    if sz.vp > sz.vfull:
        rest = jnp.concatenate(
            [wo_v[sz.vfull : nv].astype(F32), jnp.zeros((sz.vp - nv, lat), F32)], axis=0
        )
        wot[sz.vfull :] = rest.astype(BF)
    shape = (sz.vp, nv)
    same = lax.broadcasted_iota(jnp.int32, shape, 0) == lax.broadcasted_iota(jnp.int32, shape, 1)
    column = jnp.sum(jnp.where(same, vweight[...], 0.0), axis=1, keepdims=True)
    vcol[...] = jnp.broadcast_to(column, vcol.shape)

    def edges(i, carry):
        o = lax.rem(i, nx)
        c = lax.div(i, nx)
        at = pl.ds(pl.multiple_of(lax.rem(x + o, nx) * qn + c * CH, CH), CH)
        line = lax.broadcasted_iota(jnp.int32, (ext, CH), 0)
        total = jnp.zeros((ext, CH), F32)
        for k in range(slots.shape[0]):
            used = jnp.where(counts[:, at] > k, coefs[k : k + 1, at].astype(F32), 0.0)
            total = total + jnp.where(line == slots[k : k + 1, at], used, 0.0)
        st[c, :, pl.ds(pl.multiple_of(o * CH, CH), CH)] = total.astype(BF)
        return carry

    lax.fori_loop(0, nc * nx, edges, 0)
    q[...] = jnp.zeros_like(q)
    g[...] = jnp.zeros_like(g)

    def gelu_block(i):
        m = lax.rem(i, ml)
        o = lax.rem(lax.div(i, ml), nx)
        c = lax.div(i, ml * nx)
        slot = lax.rem(i, depth)
        pre_copy(i).wait()
        width = min(lat, 512)

        def some(r, carry):
            at = pl.ds(pl.multiple_of(r * 16, 16), 16)
            to = pl.ds(pl.multiple_of(o * CH + r * 16, 16), 16)
            for n in range(0, lat, width):
                v = pbuf[slot, at, n : n + width].astype(F32)
                v2_ = v * v
                t = jnp.tanh(v * (C_GELU + (C_GELU * A_GELU) * v2_))
                half = 0.5 + 0.5 * t
                hidden = v * half
                hid[c, m, to, n : n + width] = hidden.astype(BF)
                slope = half + hidden * (1.0 - half) * (2.0 * C_GELU + (6.0 * C_GELU * A_GELU) * v2_)
                dg[c, m, to, n : n + width] = slope
            return carry

        lax.fori_loop(0, CH // 16, some, 0)

        @pl.when(i + depth < blocks)
        def _():
            pre_copy(i + depth).start()

    count = float(sz.members)

    def crps_rows(c, first, at, put, n):
        weight = area[:, pl.ds(pl.multiple_of(x * qn + c * CH, CH), CH)] * vcol[at, :]
        flat = [rb.at[c, o].reshape(nv * ml, CH) for o in range(nx)]
        vals = [flat[o][pl.ds(first * ml + m, n, stride=ml), :] for o in range(nx) for m in range(ml)]
        tgt = tgt_v[c, at, :]
        pair = [jnp.zeros((n, CH), F32) for _ in vals]
        for a in range(len(vals)):
            for b in range(a + 1, len(vals)):
                sign = jnp.where(vals[a] > vals[b], 1.0, jnp.where(vals[a] < vals[b], -1.0, 0.0))
                pair[a] = pair[a] + sign
                pair[b] = pair[b] - sign
        for a in range(len(vals)):
            direct = jnp.where(vals[a] > tgt, 1.0, jnp.where(vals[a] < tgt, -1.0, 0.0))
            value = weight * (direct * (1.0 / count) - pair[a] * (1.0 / (count * (count - 1))))
            if n < 16:
                value = jnp.concatenate([value, jnp.zeros((16 - n, CH), F32)], axis=0)
            o, m = a // ml, a % ml
            if o == 0:
                dyb[c, 0, m, put, :] = value.astype(BF)
            else:
                dyo[c, o - 1, m, put, :] = value.astype(BF)

    def crps(c):
        own_copy(c).wait()
        tgt_copy(c).wait()
        for o in range(1, nx):
            forward(c, o).wait_recv()

        def some(r, carry):
            at = pl.ds(pl.multiple_of(r * 16, 16), 16)
            crps_rows(c, r * 16, at, at, 16)
            return carry

        lax.fori_loop(0, sz.vfull // 16, some, 0)
        if nv > sz.vfull:
            crps_rows(c, sz.vfull, slice(sz.vfull, nv), slice(sz.vfull, sz.vp), nv - sz.vfull)
        for o in range(1, nx):
            backward(c, o).start()

    gw = sz.gcol

    def own_columns(cc, cz):
        return pl.ds(pl.multiple_of((cc * nz + cz) * gw, gw), gw)

    g_as = [remote(ga_s.at[k], ga_r.at[k], g_s.at[k], g_r.at[k], to) for k, (_, _, to) in enumerate(group)]
    base = len(group)

    def dense(c):
        for o in range(1, nx):
            backward(c, o).wait_recv()
        dyt = [jnp.concatenate([dyb[c, o, m] for o in range(nx)], axis=1) for m in range(ml)]
        for m in range(ml):
            g[...] += dot(dyt[m], hid[c, m])

        @pl.when(c == nc - 1)
        def _():
            for k, (cz, cc, _) in enumerate(group):
                ga_s[k] = g[:, own_columns(cc, cz)].astype(BF)
                g_as[k].start()

        for m in range(ml):
            dpre = (dot(dyt[m], wot[...], ((0,), (0,))) * dg[c, m]).astype(BF)
            q[m] += dot(st[c], dpre)

    has_prev = jnp.where(s > 0, 1.0, 0.0)
    has_next = jnp.where(s < sz.grid - 1, 1.0, 0.0)

    def transpose_ext():
        lend_a.wait_recv()
        lend_b.wait_recv()

        def some(n, carry):
            at = pl.ds(pl.multiple_of(n * 128, 128), 128)
            for m in range(ml):
                table = jnp.concatenate(
                    [
                        lat_v[m, :, at].astype(F32),
                        lent_r[0, m, :, at].astype(F32) * has_prev,
                        lent_r[1, m, :, at].astype(F32) * has_next,
                    ],
                    axis=0,
                )
                turned = table.T.reshape(64 // sz.rpd, 2, sz.rpd, ext)
                for k in range(2):
                    ext_t[k, pl.ds(pl.multiple_of(n * 64, 64), 64), m * ext : (m + 1) * ext] = (
                        turned[:, k].reshape(64, ext).astype(BF)
                    )
            return carry

        lax.fori_loop(0, lat // 128, some, 0)

    def each(first, last, body):
        def one(i, carry):
            body(i)
            return carry

        lax.fori_loop(first, last, one, 0)

    group_blocks = nx * ml

    def step(t):
        @pl.when(t < nc)
        def _():
            for o in range(1, nx):
                forward(t, o).start()

        @pl.when(t < nc + 1)
        def _():
            each((t - 1) * group_blocks, (t - 1 + 1) * group_blocks, gelu_block)

        @pl.when(t == 1 + 2)
        def _():
            transpose_ext()

        @pl.when(t >= 3)
        def _():
            crps(t - 3)

    each(1, nc + 3, step)
    each(0, nc, dense)

    for m in range(ml):
        qb[m * ext : (m + 1) * ext, :] = q[m].astype(BF)
    give_a = [remote(qb.at[pl.ds(m * ext + rows, halo)], back_r.at[0, m], k_s.at[0, m], k_r.at[0, m], behind) for m in range(ml)]
    give_b = [
        remote(qb.at[pl.ds(m * ext + rows + halo, halo)], back_r.at[1, m], k_s.at[1, m], k_r.at[1, m], ahead) for m in range(ml)
    ]
    for copy in give_a + give_b:
        copy.start()
    core_copies = []
    for p, (start, width) in enumerate(sz.parts):
        score[p][...] = dot(ext_t[other], qb[:, start : start + width]).astype(BF)
        copy = remote(score[p], rcore[p], c_s.at[p], c_r.at[p], mate)
        copy.start()
        core_copies.append(copy)
    finals = g_as + core_copies + give_a + give_b

    def pick(ref, order, d):
        at = [slice(None)] * len(ref.shape)
        at[order] = d
        return ref[tuple(at)]

    for p, (start, width) in enumerate(sz.parts):
        r1[p][...] = dot(ext_t[core], qb[:, start : start + width]).reshape(nx, ny, nz, sz.rpd, width)

    def gather_sum(buf, value, axis, first):
        here = coord[axis]
        buf[here] = value.astype(buf.dtype)
        copies = []
        for o in range(1, dims[axis]):
            _, to = peer(axis, o)
            copy = remote(buf.at[here], buf.at[here], g_s.at[first + o - 1], g_r.at[first + o - 1], to)
            copy.start()
            copies.append(copy)
        return copies

    def gathered(buf, copies):
        for copy in copies:
            copy.wait_recv()
        part = buf[0].astype(F32)
        for i in range(1, buf.shape[0]):
            part = part + buf[i].astype(F32)
        return part

    part = g[:, own_columns(core, z)]
    for k, copy in enumerate(g_as):
        copy.wait_recv()
        part = part + ga_r[k].astype(F32)
    g_ys = gather_sum(gy, part, 1, base)
    base += ny - 1
    finals += g_ys

    stage1 = []
    for p, (start, width) in enumerate(sz.parts):
        core_copies[p].wait_recv()
        r1[p][...] += rcore[p][...].astype(F32).reshape(nx, ny, nz, sz.rpd, width)
        axis = AXIS_ORDERS[p][0]
        mine = []
        for o in range(1, dims[axis]):
            d, to = peer(axis, o)
            s1[p][o - 1] = pick(r1[p], axis, d).reshape(-1, width).astype(BF)
            copy = remote(s1[p].at[o - 1], v1[p].at[o - 1], a_s.at[p, 0, o - 1], a_r.at[p, 0, o - 1], to)
            copy.start()
            mine.append(copy)
        stage1.append(mine)
        finals += mine

    g_xs = gather_sum(gx, gathered(gy, g_ys), 0, base)
    base += nx - 1
    finals += g_xs

    wh_copy.wait()

    def latent_grad(m):
        give_a[m].wait_recv()
        give_b[m].wait_recv()
        line = lax.broadcasted_iota(jnp.int32, (rows, halo), 0)
        put_next = jnp.where(line == next_rows[...], has_next, 0.0).astype(BF)
        put_prev = jnp.where(line == prev_rows[...], has_prev, 0.0).astype(BF)
        whole = q[m, :rows, :] + dot(put_next, back_r[0, m]) + dot(put_prev, back_r[1, m])
        gl[m] = dot(whole.astype(BF), wh_v[...], ((1,), (1,)))
        copy = pltpu.make_async_copy(gl.at[m], out_lat.at[m], out_sem.at[m])
        copy.start()
        return copy

    outs = [latent_grad(0)]

    def stage(p, n, copies, src, got, dst, send, land):
        width = sz.parts[p][1]
        order = AXIS_ORDERS[p]
        left = sorted(order[n - 1 :])
        here = left.index(order[n - 1])
        value = pick(src[p], here, coord[order[n - 1]])
        for i, copy in enumerate(copies):
            copy.wait_recv()
            value = value + got[p][i].astype(F32).reshape(value.shape)
        dst[p][...] = value
        axis = order[n]
        here = sorted(order[n:]).index(axis)
        mine = []
        for o in range(1, dims[axis]):
            d, to = peer(axis, o)
            if send is None:
                origin = dst[p].at[d]
            else:
                send[p][o - 1] = pick(dst[p], here, d).reshape(-1, width).astype(BF)
                origin = send[p].at[o - 1]
            copy = remote(origin, land[p].at[o - 1], a_s.at[p, n, o - 1], a_r.at[p, n, o - 1], to)
            copy.start()
            mine.append(copy)
        return mine

    stage2 = [stage(p, 1, stage1[p], r1, v1, r2, s2, v2) for p in range(3)]
    for mine in stage2:
        finals += mine

    scale = 1.0 / math.sqrt(sz.total)
    gfin[core, z] = gathered(gx, g_xs) * scale
    g_bs = []
    for k, (_, _, to) in enumerate(group):
        copy = remote(gfin.at[core, z], gfin.at[core, z], g_s.at[base + k], g_r.at[base + k], to)
        copy.start()
        g_bs.append(copy)
    finals += g_bs

    for m in range(1, ml):
        outs.append(latent_grad(m))

    stage3 = [stage(p, 2, stage2[p], r2, v2, r3, None, v3) for p in range(3)]
    for mine in stage3:
        finals += mine

    for p, (start, width) in enumerate(sz.parts):
        value = r3[p][coord[AXIS_ORDERS[p][2]]]
        for i, copy in enumerate(stage3[p]):
            copy.wait_recv()
            value = value + v3[p][i]
        out_wh[:, start : start + width] = value * scale

    for copy in g_bs:
        copy.wait_recv()
    for k in range(2):
        for i in range(nz):
            at = (k * nz + i) * gw
            out_wo[:, at : at + gw] = gfin[k, i, :nv, :]

    for copy in finals + [lend_a, lend_b]:
        copy.wait_send()
    for c in range(nc):
        for o in range(1, nx):
            forward(c, o).wait_send()
            backward(c, o).wait_send()
    for copy in outs:
        copy.wait()


def shards(mesh, *args):
    predictions, target, area, var_weight, pre_act, latent, w_hidden, w_out = args[:8]
    predictions = jnp.swapaxes(predictions, 0, 1)
    w_out = w_out.T
    edge_slot, edge_count, edge_coef, send_next, send_prev = args[8:]
    sz = Sizes(mesh, predictions, pre_act, latent, send_next)
    nx, ny, nz, ml, lat, vp = sz.nx, sz.ny, sz.nz, sz.ml, sz.lat, sz.vp
    nc, ext, rows, halo = sz.nc, sz.ext, sz.rows, sz.halo
    dims = (nx, ny, nz)
    half = lat // 2

    def per_part(make):
        return [make(p, w) for p, (_, w) in enumerate(sz.parts)]

    def left(p, n):
        return [dims[a] for a in sorted(AXIS_ORDERS[p][n:])]

    def rows_of(p, n):
        return math.prod(left(p, n)) * sz.rpd

    scratch = [
        pltpu.VMEM((ml, rows, lat), BF),
        pltpu.VMEM((lat, lat), BF),
        pltpu.VMEM(w_out.shape, BF),
        pltpu.VMEM((nc, sz.nv, CH), F32),
        pltpu.VMEM((nc, nx, sz.nv, ml, CH), F32),
        pltpu.VMEM((nc, nx - 1, ml, vp, CH), BF),
        pltpu.VMEM((nc, nx, ml, vp, CH), BF),
        pltpu.VMEM((PRE_SLOTS, CH, lat), BF),
        pltpu.VMEM((nc, ml, nx * CH, lat), BF),
        pltpu.VMEM((nc, ml, nx * CH, lat), F32),
        pltpu.VMEM((nc, ext, nx * CH), BF),
        pltpu.VMEM((vp, lat), BF),
        pltpu.VMEM((vp, CH), F32),
        pltpu.VMEM((ml, ext, lat), F32),
        pltpu.VMEM((ml * ext, lat), BF),
        pltpu.VMEM((vp, lat), F32),
        pltpu.VMEM((2, half, ml * ext), BF),
        pltpu.VMEM((2, ml, halo, lat), BF),
        pltpu.VMEM((2, ml, halo, lat), BF),
        pltpu.VMEM((2, ml, halo, lat), BF),
        pltpu.VMEM((ml, rows, lat), F32),
    ]
    scratch += per_part(lambda p, w: pltpu.VMEM((half, w), BF))
    scratch += per_part(lambda p, w: pltpu.VMEM((half, w), BF))
    scratch += per_part(lambda p, w: pltpu.VMEM((nx, ny, nz, sz.rpd, w), F32))
    for n in (1, 2):
        sends = per_part(lambda p, w: pltpu.VMEM((dims[AXIS_ORDERS[p][n - 1]] - 1, rows_of(p, n), w), BF))
        lands = per_part(lambda p, w: pltpu.VMEM((dims[AXIS_ORDERS[p][n - 1]] - 1, rows_of(p, n), w), BF))
        scratch += sends + lands
        scratch += per_part(lambda p, w: pltpu.VMEM((*left(p, n), sz.rpd, w), F32))
    scratch += per_part(lambda p, w: pltpu.VMEM((dims[AXIS_ORDERS[p][2]] - 1, sz.rpd, w), F32))
    scratch += [
        pltpu.VMEM((2 * nz - 1, vp, sz.gcol), BF),
        pltpu.VMEM((2 * nz - 1, vp, sz.gcol), BF),
        pltpu.VMEM((ny, vp, sz.gcol), BF),
        pltpu.VMEM((nx, vp, sz.gcol), BF),
        pltpu.VMEM((2, nz, vp, sz.gcol), F32),
    ]
    dma = pltpu.SemaphoreType.DMA
    steps = 2 * (2 * nz - 1) + (ny - 1) + (nx - 1)
    longest = max(dims) - 1
    scratch += [
        dma((3,)),
        dma((nc,)),
        dma((PRE_SLOTS,)),
        dma((nc,)),
        dma((ml,)),
        dma((nc, nx - 1)),
        dma((nc, nx - 1)),
        dma((nc, nx - 1)),
        dma((nc, nx - 1)),
        dma((2,)),
        dma((2,)),
        dma((2, ml)),
        dma((2, ml)),
        dma((3,)),
        dma((3,)),
        dma((3, 3, longest)),
        dma((3, 3, longest)),
        dma((steps,)),
        dma((steps,)),
    ]
    anywhere = pl.BlockSpec(memory_space=pl.ANY)
    vmem = pl.BlockSpec(memory_space=pltpu.VMEM)
    grad_latent, grad_w_hidden, grad_w_out = pl.pallas_call(
        functools.partial(kernel, sz),
        out_shape=(
            jax.ShapeDtypeStruct((ml, rows, lat), F32),
            jax.ShapeDtypeStruct((sz.rpd, lat), F32),
            jax.ShapeDtypeStruct((sz.nv, lat), F32),
        ),
        in_specs=[anywhere, anywhere, vmem, vmem, anywhere, anywhere, anywhere, anywhere] + [vmem] * 5,
        out_specs=(anywhere, vmem, vmem),
        scratch_shapes=scratch,
        compiler_params=pltpu.CompilerParams(
            collective_id=0, has_side_effects=True, vmem_limit_bytes=60 * 1024 * 1024
        ),
    )(
        predictions,
        target,
        area[None, :],
        var_weight[None, :],
        pre_act,
        latent,
        w_hidden,
        w_out,
        edge_slot.T,
        edge_count[None, :],
        edge_coef.T,
        send_next[None, :],
        send_prev[None, :],
    )
    return (grad_latent, grad_w_hidden, grad_w_out.T)


def solution(mesh):
    in_specs = (
        P("member", None, "grid"),
        P(None, "grid"),
        P("grid"),
        P(),
        P("member", "grid", None),
        P("member", "grid", None),
        P(),
        P(),
        P("grid", None),
        P("grid"),
        P("grid", None),
        P("grid"),
        P("grid"),
    )
    out_specs = (P("member", "grid", None), P(("member", "grid"), None), P())
    return jax.shard_map(
        functools.partial(shards, mesh), mesh=mesh, in_specs=in_specs, out_specs=out_specs, check_vma=False
    )
```

```python
import functools
import math

import jax
import jax.numpy as jnp
from jax import lax
from jax.experimental import pallas as pl
from jax.experimental.pallas import tpu as pltpu
from jax.sharding import PartitionSpec as P

MESH_ID = pl.DeviceIdType.MESH
C_GELU = math.sqrt(2.0 / math.pi)
A_GELU = 0.044715
CH = 128
PRE_SLOTS = 8
BF = jnp.bfloat16
F32 = jnp.float32


def column_parts(lat):
    tiles = lat // 128
    sizes = [tiles // 3 + (1 if i < tiles % 3 else 0) for i in range(3)]
    parts, start = [], 0
    for size in sizes:
        parts.append((start * 128, size * 128))
        start += size
    return parts


def dot(a, b, dims=((1,), (0,))):
    return lax.dot_general(a, b, (dims, ((), ())), preferred_element_type=F32)


class Sizes:
    def __init__(self, mesh, predictions, pre_act, latent, send_next):
        self.nx = mesh.shape["member"]
        self.grid = mesh.shape["grid"]
        chips = self.grid // 2
        self.ny = math.isqrt(chips)
        self.nz = chips // self.ny
        self.nv, self.ml, self.npts = predictions.shape
        self.lat = pre_act.shape[2]
        self.rows = latent.shape[1]
        self.halo = send_next.shape[0]
        self.ext = self.rows + 2 * self.halo
        self.qn = self.npts // self.nx
        self.nc = self.qn // CH
        self.vfull = self.nv // 16 * 16
        self.vp = -(-self.nv // 16) * 16
        self.rpd = self.lat // (self.nx * self.grid)
        self.members = self.nx * self.ml
        self.gcol = self.lat // 2 // self.nz
        self.parts = column_parts(self.lat)
        self.total = self.members * self.npts * self.grid


AXIS_ORDERS = ((2, 1, 0), (1, 0, 2), (0, 2, 1))


def kernel(sz, *refs):
    it = iter(refs)
    preds, target, area, vweight, pre, latent, w_hidden, w_out = [next(it) for _ in range(8)]
    slots, counts, coefs, next_rows, prev_rows = [next(it) for _ in range(5)]
    out_lat, out_wh, out_wo = [next(it) for _ in range(3)]
    lat_v, wh_v, wo_v, tgt_v = [next(it) for _ in range(4)]
    rb, dyo, dyb, pbuf, hid, dg, st, wot, vcol = [next(it) for _ in range(9)]
    q, qb, g, ext_t = [next(it) for _ in range(4)]
    lent_s, lent_r, back_r, gl = [next(it) for _ in range(4)]
    score = [next(it) for _ in range(3)]
    rcore = [next(it) for _ in range(3)]
    r1 = [next(it) for _ in range(3)]
    s1 = [next(it) for _ in range(3)]
    v1 = [next(it) for _ in range(3)]
    r2 = [next(it) for _ in range(3)]
    s2 = [next(it) for _ in range(3)]
    v2 = [next(it) for _ in range(3)]
    r3 = [next(it) for _ in range(3)]
    v3 = [next(it) for _ in range(3)]
    ga_s, ga_r, gy, gx, gfin = [next(it) for _ in range(5)]
    loc_sem, own_sem, pre_sem, tgt_sem, out_sem = [next(it) for _ in range(5)]
    f_s, f_r, b_s, b_r, h_s, h_r, k_s, k_r = [next(it) for _ in range(8)]
    c_s, c_r, a_s, a_r, g_s, g_r = [next(it) for _ in range(6)]

    nx, ny, nz, ml, nv, lat = sz.nx, sz.ny, sz.nz, sz.ml, sz.nv, sz.lat
    nc, qn, ext, rows, halo = sz.nc, sz.qn, sz.ext, sz.rows, sz.halo
    dims = (nx, ny, nz)
    x = lax.axis_index("member")
    s = lax.axis_index("grid")
    core = lax.rem(s, 2)
    z = lax.rem(lax.div(s, 2), nz)
    y = lax.div(s, 2 * nz)
    other = 1 - core
    coord = (x, y, z)

    def device(cx, cy, cz, cc):
        return (cx, (cy * nz + cz) * 2 + cc)

    def peer(axis, by):
        there = list(coord)
        there[axis] = lax.rem(coord[axis] + by, dims[axis])
        return there[axis], device(*there, core)

    mate = device(x, y, z, other)
    group = []
    for by in range(nz):
        for swap in range(2):
            if by + swap > 0:
                there, kept = lax.rem(z + by, nz), other if swap else core
                group.append((there, kept, device(x, y, there, kept)))
    behind = (x, lax.rem(s + sz.grid - 1, sz.grid))
    ahead = (x, lax.rem(s + 1, sz.grid))

    def remote(src, dst, send_sem, recv_sem, to):
        return pltpu.make_async_remote_copy(
            src_ref=src, dst_ref=dst, send_sem=send_sem, recv_sem=recv_sem, device_id=to, device_id_type=MESH_ID
        )

    def own_copy(c):
        return pltpu.make_async_copy(
            preds.at[:, :, pl.ds(pl.multiple_of(x * qn + c * CH, CH), CH)], rb.at[c, 0], own_sem.at[c]
        )

    def tgt_copy(c):
        return pltpu.make_async_copy(
            target.at[:, pl.ds(pl.multiple_of(x * qn + c * CH, CH), CH)], tgt_v.at[c], tgt_sem.at[c]
        )

    def forward(c, o):
        there, to = peer(0, o)
        return remote(
            preds.at[:, :, pl.ds(pl.multiple_of(there * qn + c * CH, CH), CH)],
            rb.at[c, o],
            f_s.at[c, o - 1],
            f_r.at[c, o - 1],
            to,
        )

    def backward(c, o):
        _, to = peer(0, nx - o)
        return remote(dyo.at[c, o - 1], dyb.at[c, o], b_s.at[c, o - 1], b_r.at[c, o - 1], to)

    blocks = nc * nx * ml
    depth = pbuf.shape[0]

    def pre_copy(i):
        m = lax.rem(i, ml)
        o = lax.rem(lax.div(i, ml), nx)
        c = lax.div(i, ml * nx)
        quarter = lax.rem(x + o, nx)
        slot = lax.rem(i, depth)
        return pltpu.make_async_copy(
            pre.at[m, pl.ds(pl.multiple_of(quarter * qn + c * CH, CH), CH), :], pbuf.at[slot], pre_sem.at[slot]
        )

    lat_copy = pltpu.make_async_copy(latent, lat_v, loc_sem.at[0])
    wo_copy = pltpu.make_async_copy(w_out, wo_v, loc_sem.at[1])
    wh_copy = pltpu.make_async_copy(w_hidden, wh_v, loc_sem.at[2])

    lat_copy.start()
    for i in range(depth):
        pre_copy(i).start()

    wo_copy.start()
    barrier = pltpu.get_barrier_semaphore()
    neighbours = [peer(a, o)[1] for a in range(2) for o in range(1, dims[a])] + [behind, ahead]
    neighbours += [to for _, _, to in group]
    for to in neighbours:
        pl.semaphore_signal(barrier, inc=1, device_id=to, device_id_type=MESH_ID)

    pl.semaphore_wait(barrier, len(neighbours))

    for c in range(nc):
        if c < 1:
            for o in range(1, nx):
                forward(c, o).start()
        own_copy(c).start()
        tgt_copy(c).start()
    wh_copy.start()

    lat_copy.wait()
    line = lax.broadcasted_iota(jnp.int32, (rows, halo), 0)
    pick_next = jnp.where(line == next_rows[...], 1.0, 0.0).astype(BF)
    pick_prev = jnp.where(line == prev_rows[...], 1.0, 0.0).astype(BF)
    for m in range(ml):
        lent_s[0, m] = dot(pick_next, lat_v[m], ((0,), (0,))).astype(BF)
        lent_s[1, m] = dot(pick_prev, lat_v[m], ((0,), (0,))).astype(BF)
    lend_a = remote(lent_s.at[0], lent_r.at[0], h_s.at[0], h_r.at[0], ahead)
    lend_b = remote(lent_s.at[1], lent_r.at[1], h_s.at[1], h_r.at[1], behind)
    lend_a.start()
    lend_b.start()

    wo_copy.wait()
    wot[: sz.vfull] = wo_v[: sz.vfull]
    if sz.vp > sz.vfull:
        rest = jnp.concatenate(
            [wo_v[sz.vfull : nv].astype(F32), jnp.zeros((sz.vp - nv, lat), F32)], axis=0
        )
        wot[sz.vfull :] = rest.astype(BF)
    shape = (sz.vp, nv)
    same = lax.broadcasted_iota(jnp.int32, shape, 0) == lax.broadcasted_iota(jnp.int32, shape, 1)
    column = jnp.sum(jnp.where(same, vweight[...], 0.0), axis=1, keepdims=True)
    vcol[...] = jnp.broadcast_to(column, vcol.shape)

    def edges(i, carry):
        o = lax.rem(i, nx)
        c = lax.div(i, nx)
        at = pl.ds(pl.multiple_of(lax.rem(x + o, nx) * qn + c * CH, CH), CH)
        line = lax.broadcasted_iota(jnp.int32, (ext, CH), 0)
        total = jnp.zeros((ext, CH), F32)
        for k in range(slots.shape[0]):
            used = jnp.where(counts[:, at] > k, coefs[k : k + 1, at].astype(F32), 0.0)
            total = total + jnp.where(line == slots[k : k + 1, at], used, 0.0)
        st[c, :, pl.ds(pl.multiple_of(o * CH, CH), CH)] = total.astype(BF)
        return carry

    lax.fori_loop(0, nc * nx, edges, 0)
    q[...] = jnp.zeros_like(q)
    g[...] = jnp.zeros_like(g)

    def gelu_block(i):
        m = lax.rem(i, ml)
        o = lax.rem(lax.div(i, ml), nx)
        c = lax.div(i, ml * nx)
        slot = lax.rem(i, depth)
        pre_copy(i).wait()
        width = min(lat, 512)

        def some(r, carry):
            at = pl.ds(pl.multiple_of(r * 16, 16), 16)
            to = pl.ds(pl.multiple_of(o * CH + r * 16, 16), 16)
            for n in range(0, lat, width):
                v = pbuf[slot, at, n : n + width].astype(F32)
                v2_ = v * v
                t = jnp.tanh(v * (C_GELU + (C_GELU * A_GELU) * v2_))
                half = 0.5 + 0.5 * t
                hidden = v * half
                hid[c, m, to, n : n + width] = hidden.astype(BF)
                slope = half + hidden * (1.0 - half) * (2.0 * C_GELU + (6.0 * C_GELU * A_GELU) * v2_)
                dg[c, m, to, n : n + width] = slope
            return carry

        lax.fori_loop(0, CH // 16, some, 0, unroll=2)

        @pl.when(i + depth < blocks)
        def _():
            pre_copy(i + depth).start()

    count = float(sz.members)

    def crps_rows(c, first, at, put, n):
        weight = area[:, pl.ds(pl.multiple_of(x * qn + c * CH, CH), CH)] * vcol[at, :]
        flat = [rb.at[c, o].reshape(nv * ml, CH) for o in range(nx)]
        vals = [flat[o][pl.ds(first * ml + m, n, stride=ml), :] for o in range(nx) for m in range(ml)]
        tgt = tgt_v[c, at, :]
        pair = [jnp.zeros((n, CH), F32) for _ in vals]
        for a in range(len(vals)):
            for b in range(a + 1, len(vals)):
                sign = jnp.where(vals[a] > vals[b], 1.0, jnp.where(vals[a] < vals[b], -1.0, 0.0))
                pair[a] = pair[a] + sign
                pair[b] = pair[b] - sign
        for a in range(len(vals)):
            direct = jnp.where(vals[a] > tgt, 1.0, jnp.where(vals[a] < tgt, -1.0, 0.0))
            value = weight * (direct * (1.0 / count) - pair[a] * (1.0 / (count * (count - 1))))
            if n < 16:
                value = jnp.concatenate([value, jnp.zeros((16 - n, CH), F32)], axis=0)
            o, m = a // ml, a % ml
            if o == 0:
                dyb[c, 0, m, put, :] = value.astype(BF)
            else:
                dyo[c, o - 1, m, put, :] = value.astype(BF)

    def crps(c):
        own_copy(c).wait()
        tgt_copy(c).wait()
        for o in range(1, nx):
            forward(c, o).wait_recv()

        def some(r, carry):
            at = pl.ds(pl.multiple_of(r * 16, 16), 16)
            crps_rows(c, r * 16, at, at, 16)
            return carry

        lax.fori_loop(0, sz.vfull // 16, some, 0)
        if nv > sz.vfull:
            crps_rows(c, sz.vfull, slice(sz.vfull, nv), slice(sz.vfull, sz.vp), nv - sz.vfull)
        for o in range(1, nx):
            backward(c, o).start()

    gw = sz.gcol

    def own_columns(cc, cz):
        return pl.ds(pl.multiple_of((cc * nz + cz) * gw, gw), gw)

    g_as = [remote(ga_s.at[k], ga_r.at[k], g_s.at[k], g_r.at[k], to) for k, (_, _, to) in enumerate(group)]
    base = len(group)

    def dense(c):
        for o in range(1, nx):
            backward(c, o).wait_recv()
        dyt = [jnp.concatenate([dyb[c, o, m] for o in range(nx)], axis=1) for m in range(ml)]
        for m in range(ml):
            g[...] += dot(dyt[m], hid[c, m])

        @pl.when(c == nc - 1)
        def _():
            for k, (cz, cc, _) in enumerate(group):
                ga_s[k] = g[:, own_columns(cc, cz)].astype(BF)
                g_as[k].start()

        for m in range(ml):
            dpre = (dot(dyt[m], wot[...], ((0,), (0,))) * dg[c, m]).astype(BF)
            q[m] += dot(st[c], dpre)

    has_prev = jnp.where(s > 0, 1.0, 0.0)
    has_next = jnp.where(s < sz.grid - 1, 1.0, 0.0)

    def transpose_ext():
        lend_a.wait_recv()
        lend_b.wait_recv()

        def some(n, carry):
            at = pl.ds(pl.multiple_of(n * 128, 128), 128)
            for m in range(ml):
                table = jnp.concatenate(
                    [
                        lat_v[m, :, at].astype(F32),
                        lent_r[0, m, :, at].astype(F32) * has_prev,
                        lent_r[1, m, :, at].astype(F32) * has_next,
                    ],
                    axis=0,
                )
                turned = table.T.reshape(64 // sz.rpd, 2, sz.rpd, ext)
                for k in range(2):
                    ext_t[k, pl.ds(pl.multiple_of(n * 64, 64), 64), m * ext : (m + 1) * ext] = (
                        turned[:, k].reshape(64, ext).astype(BF)
                    )
            return carry

        lax.fori_loop(0, lat // 128, some, 0)

    def each(first, last, body):
        def one(i, carry):
            body(i)
            return carry

        lax.fori_loop(first, last, one, 0)

    group_blocks = nx * ml

    def step(t):
        @pl.when(t < nc)
        def _():
            for o in range(1, nx):
                forward(t, o).start()

        @pl.when(t < nc + 1)
        def _():
            each((t - 1) * group_blocks, (t - 1 + 1) * group_blocks, gelu_block)

        @pl.when(t == 1 + 2)
        def _():
            transpose_ext()

        @pl.when(t >= 3)
        def _():
            crps(t - 3)

    each(1, nc + 3, step)
    each(0, nc, dense)

    for m in range(ml):
        qb[m * ext : (m + 1) * ext, :] = q[m].astype(BF)
    give_a = [remote(qb.at[pl.ds(m * ext + rows, halo)], back_r.at[0, m], k_s.at[0, m], k_r.at[0, m], behind) for m in range(ml)]
    give_b = [
        remote(qb.at[pl.ds(m * ext + rows + halo, halo)], back_r.at[1, m], k_s.at[1, m], k_r.at[1, m], ahead) for m in range(ml)
    ]
    for copy in give_a + give_b:
        copy.start()
    core_copies = []
    for p, (start, width) in enumerate(sz.parts):
        score[p][...] = dot(ext_t[other], qb[:, start : start + width]).astype(BF)
        copy = remote(score[p], rcore[p], c_s.at[p], c_r.at[p], mate)
        copy.start()
        core_copies.append(copy)
    finals = g_as + core_copies + give_a + give_b

    def pick(ref, order, d):
        at = [slice(None)] * len(ref.shape)
        at[order] = d
        return ref[tuple(at)]

    for p, (start, width) in enumerate(sz.parts):
        r1[p][...] = dot(ext_t[core], qb[:, start : start + width]).reshape(nx, ny, nz, sz.rpd, width)

    def gather_sum(buf, value, axis, first):
        here = coord[axis]
        buf[here] = value.astype(buf.dtype)
        copies = []
        for o in range(1, dims[axis]):
            _, to = peer(axis, o)
            copy = remote(buf.at[here], buf.at[here], g_s.at[first + o - 1], g_r.at[first + o - 1], to)
            copy.start()
            copies.append(copy)
        return copies

    def gathered(buf, copies):
        for copy in copies:
            copy.wait_recv()
        part = buf[0].astype(F32)
        for i in range(1, buf.shape[0]):
            part = part + buf[i].astype(F32)
        return part

    part = g[:, own_columns(core, z)]
    for k, copy in enumerate(g_as):
        copy.wait_recv()
        part = part + ga_r[k].astype(F32)
    g_ys = gather_sum(gy, part, 1, base)
    base += ny - 1
    finals += g_ys

    stage1 = []
    for p, (start, width) in enumerate(sz.parts):
        core_copies[p].wait_recv()
        r1[p][...] += rcore[p][...].astype(F32).reshape(nx, ny, nz, sz.rpd, width)
        axis = AXIS_ORDERS[p][0]
        mine = []
        for o in range(1, dims[axis]):
            d, to = peer(axis, o)
            s1[p][o - 1] = pick(r1[p], axis, d).reshape(-1, width).astype(BF)
            copy = remote(s1[p].at[o - 1], v1[p].at[o - 1], a_s.at[p, 0, o - 1], a_r.at[p, 0, o - 1], to)
            copy.start()
            mine.append(copy)
        stage1.append(mine)
        finals += mine

    g_xs = gather_sum(gx, gathered(gy, g_ys), 0, base)
    base += nx - 1
    finals += g_xs

    wh_copy.wait()

    def latent_grad(m):
        give_a[m].wait_recv()
        give_b[m].wait_recv()
        line = lax.broadcasted_iota(jnp.int32, (rows, halo), 0)
        put_next = jnp.where(line == next_rows[...], has_next, 0.0).astype(BF)
        put_prev = jnp.where(line == prev_rows[...], has_prev, 0.0).astype(BF)
        whole = q[m, :rows, :] + dot(put_next, back_r[0, m]) + dot(put_prev, back_r[1, m])
        gl[m] = dot(whole.astype(BF), wh_v[...], ((1,), (1,)))
        copy = pltpu.make_async_copy(gl.at[m], out_lat.at[m], out_sem.at[m])
        copy.start()
        return copy

    outs = [latent_grad(0)]

    def stage(p, n, copies, src, got, dst, send, land):
        width = sz.parts[p][1]
        order = AXIS_ORDERS[p]
        left = sorted(order[n - 1 :])
        here = left.index(order[n - 1])
        value = pick(src[p], here, coord[order[n - 1]])
        for i, copy in enumerate(copies):
            copy.wait_recv()
            value = value + got[p][i].astype(F32).reshape(value.shape)
        dst[p][...] = value
        axis = order[n]
        here = sorted(order[n:]).index(axis)
        mine = []
        for o in range(1, dims[axis]):
            d, to = peer(axis, o)
            if send is None:
                origin = dst[p].at[d]
            else:
                send[p][o - 1] = pick(dst[p], here, d).reshape(-1, width).astype(BF)
                origin = send[p].at[o - 1]
            copy = remote(origin, land[p].at[o - 1], a_s.at[p, n, o - 1], a_r.at[p, n, o - 1], to)
            copy.start()
            mine.append(copy)
        return mine

    stage2 = [stage(p, 1, stage1[p], r1, v1, r2, s2, v2) for p in range(3)]
    for mine in stage2:
        finals += mine

    scale = 1.0 / math.sqrt(sz.total)
    gfin[core, z] = gathered(gx, g_xs) * scale
    g_bs = []
    for k, (_, _, to) in enumerate(group):
        copy = remote(gfin.at[core, z], gfin.at[core, z], g_s.at[base + k], g_r.at[base + k], to)
        copy.start()
        g_bs.append(copy)
    finals += g_bs

    for m in range(1, ml):
        outs.append(latent_grad(m))

    stage3 = [stage(p, 2, stage2[p], r2, v2, r3, None, v3) for p in range(3)]
    for mine in stage3:
        finals += mine

    for p, (start, width) in enumerate(sz.parts):
        value = r3[p][coord[AXIS_ORDERS[p][2]]]
        for i, copy in enumerate(stage3[p]):
            copy.wait_recv()
            value = value + v3[p][i]
        out_wh[:, start : start + width] = value * scale

    for copy in g_bs:
        copy.wait_recv()
    for k in range(2):
        for i in range(nz):
            at = (k * nz + i) * gw
            out_wo[:, at : at + gw] = gfin[k, i, :nv, :]

    for copy in finals + [lend_a, lend_b]:
        copy.wait_send()
    for c in range(nc):
        for o in range(1, nx):
            forward(c, o).wait_send()
            backward(c, o).wait_send()
    for copy in outs:
        copy.wait()


def shards(mesh, *args):
    predictions, target, area, var_weight, pre_act, latent, w_hidden, w_out = args[:8]
    predictions = jnp.swapaxes(predictions, 0, 1)
    w_out = w_out.T
    edge_slot, edge_count, edge_coef, send_next, send_prev = args[8:]
    sz = Sizes(mesh, predictions, pre_act, latent, send_next)
    nx, ny, nz, ml, lat, vp = sz.nx, sz.ny, sz.nz, sz.ml, sz.lat, sz.vp
    nc, ext, rows, halo = sz.nc, sz.ext, sz.rows, sz.halo
    dims = (nx, ny, nz)
    half = lat // 2

    def per_part(make):
        return [make(p, w) for p, (_, w) in enumerate(sz.parts)]

    def left(p, n):
        return [dims[a] for a in sorted(AXIS_ORDERS[p][n:])]

    def rows_of(p, n):
        return math.prod(left(p, n)) * sz.rpd

    scratch = [
        pltpu.VMEM((ml, rows, lat), BF),
        pltpu.VMEM((lat, lat), BF),
        pltpu.VMEM(w_out.shape, BF),
        pltpu.VMEM((nc, sz.nv, CH), F32),
        pltpu.VMEM((nc, nx, sz.nv, ml, CH), F32),
        pltpu.VMEM((nc, nx - 1, ml, vp, CH), BF),
        pltpu.VMEM((nc, nx, ml, vp, CH), BF),
        pltpu.VMEM((PRE_SLOTS, CH, lat), BF),
        pltpu.VMEM((nc, ml, nx * CH, lat), BF),
        pltpu.VMEM((nc, ml, nx * CH, lat), F32),
        pltpu.VMEM((nc, ext, nx * CH), BF),
        pltpu.VMEM((vp, lat), BF),
        pltpu.VMEM((vp, CH), F32),
        pltpu.VMEM((ml, ext, lat), F32),
        pltpu.VMEM((ml * ext, lat), BF),
        pltpu.VMEM((vp, lat), F32),
        pltpu.VMEM((2, half, ml * ext), BF),
        pltpu.VMEM((2, ml, halo, lat), BF),
        pltpu.VMEM((2, ml, halo, lat), BF),
        pltpu.VMEM((2, ml, halo, lat), BF),
        pltpu.VMEM((ml, rows, lat), F32),
    ]
    scratch += per_part(lambda p, w: pltpu.VMEM((half, w), BF))
    scratch += per_part(lambda p, w: pltpu.VMEM((half, w), BF))
    scratch += per_part(lambda p, w: pltpu.VMEM((nx, ny, nz, sz.rpd, w), F32))
    for n in (1, 2):
        sends = per_part(lambda p, w: pltpu.VMEM((dims[AXIS_ORDERS[p][n - 1]] - 1, rows_of(p, n), w), BF))
        lands = per_part(lambda p, w: pltpu.VMEM((dims[AXIS_ORDERS[p][n - 1]] - 1, rows_of(p, n), w), BF))
        scratch += sends + lands
        scratch += per_part(lambda p, w: pltpu.VMEM((*left(p, n), sz.rpd, w), F32))
    scratch += per_part(lambda p, w: pltpu.VMEM((dims[AXIS_ORDERS[p][2]] - 1, sz.rpd, w), F32))
    scratch += [
        pltpu.VMEM((2 * nz - 1, vp, sz.gcol), BF),
        pltpu.VMEM((2 * nz - 1, vp, sz.gcol), BF),
        pltpu.VMEM((ny, vp, sz.gcol), BF),
        pltpu.VMEM((nx, vp, sz.gcol), BF),
        pltpu.VMEM((2, nz, vp, sz.gcol), F32),
    ]
    dma = pltpu.SemaphoreType.DMA
    steps = 2 * (2 * nz - 1) + (ny - 1) + (nx - 1)
    longest = max(dims) - 1
    scratch += [
        dma((3,)),
        dma((nc,)),
        dma((PRE_SLOTS,)),
        dma((nc,)),
        dma((ml,)),
        dma((nc, nx - 1)),
        dma((nc, nx - 1)),
        dma((nc, nx - 1)),
        dma((nc, nx - 1)),
        dma((2,)),
        dma((2,)),
        dma((2, ml)),
        dma((2, ml)),
        dma((3,)),
        dma((3,)),
        dma((3, 3, longest)),
        dma((3, 3, longest)),
        dma((steps,)),
        dma((steps,)),
    ]
    anywhere = pl.BlockSpec(memory_space=pl.ANY)
    vmem = pl.BlockSpec(memory_space=pltpu.VMEM)
    grad_latent, grad_w_hidden, grad_w_out = pl.pallas_call(
        functools.partial(kernel, sz),
        out_shape=(
            jax.ShapeDtypeStruct((ml, rows, lat), F32),
            jax.ShapeDtypeStruct((sz.rpd, lat), F32),
            jax.ShapeDtypeStruct((sz.nv, lat), F32),
        ),
        in_specs=[anywhere, anywhere, vmem, vmem, anywhere, anywhere, anywhere, anywhere] + [vmem] * 5,
        out_specs=(anywhere, vmem, vmem),
        scratch_shapes=scratch,
        compiler_params=pltpu.CompilerParams(
            collective_id=0, has_side_effects=True, vmem_limit_bytes=60 * 1024 * 1024
        ),
    )(
        predictions,
        target,
        area[None, :],
        var_weight[None, :],
        pre_act,
        latent,
        w_hidden,
        w_out,
        edge_slot.T,
        edge_count[None, :],
        edge_coef.T,
        send_next[None, :],
        send_prev[None, :],
    )
    return (grad_latent, grad_w_hidden, grad_w_out.T)


def solution(mesh):
    in_specs = (
        P("member", None, "grid"),
        P(None, "grid"),
        P("grid"),
        P(),
        P("member", "grid", None),
        P("member", "grid", None),
        P(),
        P(),
        P("grid", None),
        P("grid"),
        P("grid", None),
        P("grid"),
        P("grid"),
    )
    out_specs = (P("member", "grid", None), P(("member", "grid"), None), P())
    return jax.shard_map(
        functools.partial(shards, mesh), mesh=mesh, in_specs=in_specs, out_specs=out_specs, check_vma=False
    )
```
